128 devices in a mesh: blk: 32 (over z, x_hi, y), col: 4 (over x_lo, core).
Axes of the slice: x: 4 (x_hi: 2, x_lo: 2; x = x_hi * 2 + x_lo), y: 4, z: 4, core: 2. Of those that a mesh axis runs over, the one named last changes fastest.
Arguments:
- worker_emb: float32 [65536, 256], P('blk', 'col'), may hold values from -24 to 24
- job_emb: float32 [8192, 256], P('blk', 'col'), may hold values from -48 to 48
- worker_cot: float32 [65536, 256], P('blk', 'col'), may hold values from -24 to 24
- job_cot: float32 [8192, 256], P('blk', 'col'), may hold values from -48 to 48
- worker_deg: int32 [65536], P('blk'), may hold values from 1 to 65568, as said below
- job_deg: int32 [8192], P('blk'), may hold values from 1 to 2097184, as said below
- block_rows: int32 [16384], P(('blk', 'col')), may hold values from 0 to 15, as said below
- block_cols: int32 [16384], P(('blk', 'col')), may hold values from 0 to 63
- block_tiles: int32 [16384, 128, 128], P(('blk', 'col')), may hold values from 0 to 1
- live_count: int32 [32, 4], P('blk', 'col'), may hold values from 16 to 128, as said below
Outputs:
- worker_out: float32 [65536, 256], P('blk', 'col')
- job_out: float32 [8192, 256], P('blk', 'col')
- worker_grad: float32 [65536, 256], P('blk', 'col')
- job_grad: float32 [8192, 256], P('blk', 'col')
The draws below stay inside these ranges and needn't reach their ends.
Inputs may be any that keep to these rules, and one draw needn't show every extreme that they name: `block_rows`: worker block row within the 16 row blocks of the slot's blk index. `live_count`: slots from this count on are ignored; some device has all 128 slots live. `worker_deg`: at least the worker's number of edges in A. `job_deg`: at least the job's number of edges in A.
All inputs are finite; a program needn't handle non-finite values.
Results may differ from the reference program's by a relative error of at most 0.0029.
Values may be sent and summed in bfloat16 or wider, within the bound.
A program may use at most 128 MiB of HBM per device.

```python
import jax
import jax.numpy as jnp
from jax import lax

E = 256
TILE = 128
NB = 128
RB = 16
NW = 65536
NJ = 8192
NJB = 64
SLOTS = 16384
N_BLK = 32
N_COL = 4


def window_graph(key):
    rows_key, cols_key, tiles_key, live_key, full_key, wrest_key, jrest_key, wtop_key, jtop_key = jax.random.split(key, 9)
    counts = jax.random.randint(live_key, (N_BLK * N_COL,), NB // 8, NB + 1)
    full_slot = jax.random.randint(full_key, (), 0, N_BLK * N_COL)
    counts = jnp.where(jnp.arange(N_BLK * N_COL) == full_slot, NB, counts).astype(jnp.int32)
    block_rows = jax.random.randint(rows_key, (SLOTS,), 0, RB).astype(jnp.int32)
    block_cols = jax.random.randint(cols_key, (SLOTS,), 0, NJB).astype(jnp.int32)
    tiles = (jax.random.randint(tiles_key, (SLOTS, TILE, TILE), 0, 64) == 0).astype(jnp.int32)
    live = (jnp.arange(NB)[None, :] < counts[:, None]).reshape(SLOTS).astype(jnp.int32)
    row_edges = jnp.sum(tiles, axis=2) * live[:, None]
    col_edges = jnp.sum(tiles, axis=1) * live[:, None]
    owner_blk = jnp.arange(SLOTS) // (N_COL * NB)
    worker_block = owner_blk * RB + block_rows
    worker_window = jax.ops.segment_sum(row_edges, worker_block, num_segments=N_BLK * RB).reshape(NW)
    job_window = jax.ops.segment_sum(col_edges, block_cols, num_segments=NJB).reshape(NJ)
    worker_deg = worker_window + jax.random.randint(wrest_key, (NW,), 1, 33)
    job_deg = job_window + jax.random.randint(jrest_key, (NJ,), 1, 33)
    worker_top = jax.random.randint(wtop_key, (), 0, NW)
    job_top = jax.random.randint(jtop_key, (), 0, NJ)
    worker_deg = jnp.where(jnp.arange(NW) == worker_top, N_COL * NB * TILE + 32, worker_deg)
    job_deg = jnp.where(jnp.arange(NJ) == job_top, SLOTS * TILE + 32, job_deg)
    return (block_rows, block_cols, tiles, counts.reshape(N_BLK, N_COL), worker_deg.astype(jnp.int32), job_deg.astype(jnp.int32))


def draw_block_rows(key, part):
    return window_graph(key)[0]


def draw_block_cols(key, part):
    return window_graph(key)[1]


def draw_block_tiles(key, part):
    return window_graph(key)[2]


def draw_live_count(key, part):
    return window_graph(key)[3]


def draw_worker_deg(key, part):
    return window_graph(key)[4]


def draw_job_deg(key, part):
    return window_graph(key)[5]


def level_of(rng, dims, pieces, least, largest):
    gain = 1.0
    for position, parts in pieces:
        draws = jax.random.uniform(jax.random.fold_in(jax.random.fold_in(rng, 6), position), (parts,), jnp.float32, least / len(pieces), largest / len(pieces))
        gain = gain * jnp.repeat(jnp.exp(draws), dims[position] // parts).reshape((-1,) + (1,) * (len(dims) - 1 - position))
    return gain


def gaussian(own_key, shape, spread, bound, shards=(), kind=jnp.bfloat16):
    entries = spread * jax.random.normal(own_key, shape, jnp.float32)
    if shards:
        entries = entries * level_of(own_key, shape, shards, -0.22, 0.18)
    return jnp.clip(entries, -bound, bound).astype(kind)


def setup_inputs(seed: int = 0) -> dict:
    keys = jax.random.split(jax.random.key(seed), 11)
    worker_emb = gaussian(keys[0], (NW, E), 4.0, 24.0, ((0, 32), (1, 4)), jnp.float32)
    job_emb = gaussian(keys[1], (NJ, E), 8.0, 48.0, ((0, 32), (1, 4)), jnp.float32)
    worker_cot = gaussian(keys[2], (NW, E), 4.0, 24.0, ((0, 32), (1, 4)), jnp.float32)
    job_cot = gaussian(keys[3], (NJ, E), 8.0, 48.0, ((0, 32), (1, 4)), jnp.float32)
    worker_deg = draw_worker_deg(jax.random.fold_in(keys[10], 71), 0)
    job_deg = draw_job_deg(jax.random.fold_in(keys[10], 71), 0)
    block_rows = draw_block_rows(jax.random.fold_in(keys[10], 71), 0)
    block_cols = draw_block_cols(jax.random.fold_in(keys[10], 71), 0)
    block_tiles = draw_block_tiles(jax.random.fold_in(keys[10], 71), 0)
    live_count = draw_live_count(jax.random.fold_in(keys[10], 71), 0)
    return {"worker_emb": worker_emb, "job_emb": job_emb, "worker_cot": worker_cot, "job_cot": job_cot, "worker_deg": worker_deg, "job_deg": job_deg, "block_rows": block_rows, "block_cols": block_cols, "block_tiles": block_tiles, "live_count": live_count}


def reference(worker_emb, job_emb, worker_cot, job_cot, worker_deg, job_deg, block_rows, block_cols, block_tiles, live_count):
    worker_scale = lax.rsqrt(worker_deg.astype(jnp.float32))[:, None]
    job_scale = lax.rsqrt(job_deg.astype(jnp.float32))[:, None]
    worker_src = jnp.concatenate([worker_emb * worker_scale, worker_cot * worker_scale], axis=1).astype(jnp.bfloat16)
    job_src = jnp.concatenate([job_emb * job_scale, job_cot * job_scale], axis=1).astype(jnp.bfloat16)
    width = 2 * E
    job_blocked = job_src.astype(jnp.float32).reshape(NJB, TILE, width)
    worker_parts = worker_src.astype(jnp.float32).reshape(N_BLK, RB, TILE, width)
    rows_all = block_rows.reshape(N_BLK, N_COL, NB)
    cols_all = block_cols.reshape(N_BLK, N_COL, NB)
    tiles_all = block_tiles.reshape(N_BLK, N_COL, NB, TILE, TILE)

    def shard_step(job_total, inputs):
        rows_here, cols_here, tiles_here, live_here, worker_here = inputs
        worker_total = jnp.zeros((RB, TILE, width), jnp.float32)
        for column in range(N_COL):
            live_mask = jnp.arange(NB) < live_here[column]
            dense = jnp.where(live_mask[:, None, None], tiles_here[column], 0).astype(jnp.float32)
            gathered = job_blocked[cols_here[column]]
            product = jnp.einsum('sij,sjk->sik', dense, gathered, precision=lax.Precision.HIGHEST)
            worker_total = worker_total + jax.ops.segment_sum(product, rows_here[column], num_segments=RB)
            picked = worker_here[rows_here[column]]
            flipped = jnp.einsum('sji,sjk->sik', dense, picked, precision=lax.Precision.HIGHEST)
            job_total = job_total + jax.ops.segment_sum(flipped, cols_here[column], num_segments=NJB)
        return (job_total, worker_total)
    start_total = jnp.zeros((NJB, TILE, width), jnp.float32)
    job_total, worker_totals = lax.scan(shard_step, start_total, (rows_all, cols_all, tiles_all, live_count, worker_parts))
    worker_sum = worker_totals.reshape(NW, width)
    job_sum = job_total.reshape(NJ, width)
    worker_out = worker_scale * worker_sum[:, :E]
    worker_grad = worker_scale * worker_sum[:, E:]
    job_out = job_scale * job_sum[:, :E]
    job_grad = job_scale * job_sum[:, E:]
    return (worker_out, job_out, worker_grad, job_grad)
```

```python
import functools

import jax
import jax.numpy as jnp
from jax import lax
from jax.experimental import pallas as pl
from jax.experimental.pallas import tpu as pltpu
from jax.sharding import PartitionSpec as P

MESH = pl.DeviceIdType.MESH
TILE = 128
NB = 128
RB = 16
NJB = 64
NW_LOC = RB * TILE
NJ = NJB * TILE
JLOC = 256
PARTS = ((0, 96, "xyz"), (96, 80, "yzx"), (176, 80, "zxy"))
DIMS = (("x", 2), ("z", 4), ("x", 2), ("y", 4))
TCHUNK = 8
NCHUNK = NB // TCHUNK
NBUF = 4
KCHUNK = 32
GROUP = 16


def position():
    blk = lax.axis_index("blk")
    col = lax.axis_index("col")
    return {
        "z": blk // 8,
        "x": ((blk // 4) % 2) * 2 + col // 2,
        "y": blk % 4,
        "core": col % 2,
    }


def device(at):
    x = at["x"]
    return (at["z"] * 8 + (x // 2) * 4 + at["y"], (x % 2) * 2 + at["core"])


def shifted(at, axis, by):
    return {**at, axis: (at[axis] + by + 4) % 4}


def neighbours(at):
    out = [device(shifted(at, axis, d)) for axis in "xyz" for d in (1, 2, 3)]
    out.append(device({**at, "core": 1 - at["core"]}))
    return out


def greet(at):
    barrier = pltpu.get_barrier_semaphore()
    others = neighbours(at)
    for other in others:
        pl.semaphore_signal(barrier, inc=1, device_id=other, device_id_type=MESH)
    pl.semaphore_wait(barrier, len(others))


def dims_of(axes):
    return tuple(n for name, n in DIMS if name in axes)


def pick(axes, fixed):
    index = []
    seen_x = False
    for name, _ in DIMS:
        if name not in axes:
            continue
        if name not in fixed:
            index.append(slice(None))
        elif name == "x":
            index.append(fixed["x"] // 2 if seen_x else fixed["x"] % 2)
        else:
            index.append(fixed[name])
        if name == "x":
            seen_x = True
    return tuple(index)


def gather_kernel(
    wsrc,
    jsrc,
    tiles,
    meta,
    table,
    workers,
    tiles_out,
    meta_out,
    tin,
    tb,
    tin_sem,
    tsend,
    trecv,
    tlocal,
    gsend,
    grecv,
    osend,
    orecv,
    olocal,
):
    at = position()
    x_lo = at["x"] % 2
    core = at["core"]

    def load(i):
        return pltpu.make_async_copy(
            tiles.at[pl.ds(i * TCHUNK, TCHUNK)], tin.at[i % NBUF], tin_sem.at[i % NBUF]
        )

    for i in range(NBUF):
        load(i).start()
    local = [
        pltpu.make_async_copy(jsrc, table.at[pick("xyz", at)], olocal.at[0]),
        pltpu.make_async_copy(wsrc, workers.at[x_lo], olocal.at[1]),
        pltpu.make_async_copy(meta, meta_out.at[core], olocal.at[2]),
    ]
    for c in local:
        c.start()
    greet(at)

    def remote(src, dst, sems, rems, i, target):
        c = pltpu.make_async_remote_copy(
            src_ref=src,
            dst_ref=dst,
            send_sem=sems.at[i],
            recv_sem=rems.at[i],
            device_id=device(target),
            device_id_type=MESH,
        )
        c.start()
        return c

    def rows(p):
        return pl.ds(PARTS[p][0], PARTS[p][1])

    def piece(p, fixed):
        return table.at[pick("xyz", fixed) + (rows(p), slice(None))]

    first, second, third = {}, {}, {}
    for p in range(3):
        a1, a2, a3 = PARTS[p][2]
        for d in (1, 2, 3):
            first[p, d] = remote(
                jsrc.at[rows(p)], piece(p, at), gsend, grecv, p * 18 + d - 1, shifted(at, a1, d)
            )
    partner = {**at, "core": 1 - core}
    mcopy = remote(meta, meta_out.at[core], osend, orecv, 0, partner)
    wcopy = remote(wsrc, workers.at[x_lo], osend, orecv, 1, {**at, "x": at["x"] + 1 - 2 * x_lo})

    tcopies = []

    def chunk(i):
        load(i).wait()
        tb[pl.ds(i * TCHUNK, TCHUNK)] = tin[i % NBUF].astype(jnp.float32).astype(jnp.bfloat16)
        if i + NBUF < NCHUNK:
            load(i + NBUF).start()
        here = tb.at[pl.ds(i * TCHUNK, TCHUNK)]
        there = tiles_out.at[core, pl.ds(i * TCHUNK, TCHUNK)]
        tcopies.append(remote(here, there, tsend, trecv, i, partner))
        c = pltpu.make_async_copy(here, there, tlocal.at[i])
        c.start()
        local.append(c)

    for i in range(4):
        chunk(i)
    local[0].wait()
    for p in range(3):
        a1, a2, a3 = PARTS[p][2]
        for d in (1, 2, 3):
            first[p, d].wait_recv()
        own = piece(p, {a2: at[a2], a3: at[a3]})
        for d in (1, 2, 3):
            second[p, d] = remote(own, own, gsend, grecv, p * 18 + 3 + d - 1, shifted(at, a2, d))
    for p in range(3):
        a1, a2, a3 = PARTS[p][2]
        own = piece(p, {a2: at[a2], a3: at[a3]})
        for d in (1, 2, 3):
            third[p, 0, d] = remote(own, own, gsend, grecv, p * 18 + 6 + d - 1, shifted(at, a3, d))
    for i in range(4, 8):
        chunk(i)
    for g in (1, 3, 2):
        for p in range(3):
            a1, a2, a3 = PARTS[p][2]
            second[p, g].wait_recv()
            got = piece(p, {a2: (at[a2] - g + 4) % 4, a3: at[a3]})
            for d in (1, 2, 3):
                third[p, g, d] = remote(
                    got, got, gsend, grecv, p * 18 + 6 + g * 3 + d - 1, shifted(at, a3, d)
                )
    for i in range(8, NCHUNK):
        chunk(i)
    for c in local[1:]:
        c.wait()
    mcopy.wait()
    wcopy.wait()
    for c in tcopies:
        c.wait()
    for c in list(first.values()) + list(second.values()):
        c.wait_send()
    for c in third.values():
        c.wait()


def gather(wsrc, jsrc, tiles, meta):
    hbm = pl.BlockSpec(memory_space=pl.ANY)
    return pl.pallas_call(
        gather_kernel,
        in_specs=[hbm] * 4,
        out_specs=[hbm] * 4,
        out_shape=[
            jax.ShapeDtypeStruct(dims_of("xyz") + (JLOC, TILE), jnp.bfloat16),
            jax.ShapeDtypeStruct((2, NW_LOC, TILE), jnp.bfloat16),
            jax.ShapeDtypeStruct((2, NB, TILE, TILE), jnp.bfloat16),
            jax.ShapeDtypeStruct((2, 8, TILE), jnp.int32),
        ],
        scratch_shapes=[
            pltpu.VMEM((NBUF, TCHUNK, TILE, TILE), jnp.int32),
            pltpu.VMEM((NB, TILE, TILE), jnp.bfloat16),
            pltpu.SemaphoreType.DMA((NBUF,)),
            pltpu.SemaphoreType.DMA((NCHUNK,)),
            pltpu.SemaphoreType.DMA((NCHUNK,)),
            pltpu.SemaphoreType.DMA((NCHUNK,)),
            pltpu.SemaphoreType.DMA((54,)),
            pltpu.SemaphoreType.DMA((54,)),
            pltpu.SemaphoreType.DMA((2,)),
            pltpu.SemaphoreType.DMA((2,)),
            pltpu.SemaphoreType.DMA((3,)),
        ],
        compiler_params=pltpu.CompilerParams(
            collective_id=0, has_side_effects=True, vmem_limit_bytes=56 * 2**20
        ),
        name="gather_all",
    )(wsrc, jsrc, tiles, meta)


def sparse_kernel(
    meta, table, workers, tiles, jobs_out, away_out, home_out, tbuf, wbuf, xbuf, jacc, wacc, jbf, abf, sems, tsems, osems
):
    def tile_load(k):
        return pltpu.make_async_copy(
            tiles.at[pl.ds(k * KCHUNK, KCHUNK)], xbuf.at[pl.ds(k * KCHUNK, KCHUNK)], tsems.at[k]
        )

    wload = pltpu.make_async_copy(workers, wbuf, sems.at[0])
    tload = pltpu.make_async_copy(table, tbuf, sems.at[1])
    wload.start()
    tload.start()

    @pl.loop(0, 2 * NB // KCHUNK)
    def _(k):
        tile_load(k).start()

    @pl.loop(0, NJB)
    def _(j):
        jacc[:, pl.ds(j * TILE, TILE), :] = jnp.zeros((2, TILE, TILE), jnp.float32)

    @pl.loop(0, RB)
    def _(j):
        wacc[:, pl.ds(j * TILE, TILE), :] = jnp.zeros((2, TILE, TILE), jnp.float32)

    wload.wait()
    tload.wait()

    @pl.loop(0, 2 * NB // KCHUNK)
    def _(k):
        tile_load(k).wait()
        half = k // (NB // KCHUNK)
        live = meta[half, 2, 0]

        @pl.loop(0, KCHUNK // GROUP)
        def _(q):
            start = (k % (NB // KCHUNK)) * KCHUNK + q * GROUP

            @pl.when(start < live)
            def _():
                for g in range(GROUP):
                    s = start + g
                    r = pl.multiple_of(meta[half, 0, s] * TILE, TILE)
                    c = pl.multiple_of(meta[half, 1, s] * TILE, TILE)
                    tile = xbuf[half * NB + s]
                    tile = jnp.where(s < live, tile, jnp.zeros_like(tile))
                    jb = jnp.concatenate(
                        [tbuf[0, pl.ds(c, TILE), :], tbuf[1, pl.ds(c, TILE), :]], axis=1
                    )
                    f = jnp.dot(tile, jb, preferred_element_type=jnp.float32)
                    wacc[0, pl.ds(r, TILE), :] += f[:, :TILE]
                    wacc[1, pl.ds(r, TILE), :] += f[:, TILE:]
                    wb = jnp.concatenate(
                        [wbuf[0, pl.ds(r, TILE), :], wbuf[1, pl.ds(r, TILE), :]], axis=1
                    )
                    t = lax.dot_general(
                        tile, wb, (((0,), (0,)), ((), ())), preferred_element_type=jnp.float32
                    )
                    jacc[0, pl.ds(c, TILE), :] += t[:, :TILE]
                    jacc[1, pl.ds(c, TILE), :] += t[:, TILE:]

    x_lo = meta[0, 3, 0]

    @pl.loop(0, RB)
    def _(j):
        here = pl.ds(j * TILE, TILE)
        abf[here, :] = wacc[1 - x_lo, here, :].astype(jnp.bfloat16)

    outs = [
        pltpu.make_async_copy(wacc.at[x_lo], home_out, osems.at[0]),
        pltpu.make_async_copy(abf, away_out, osems.at[1]),
    ]
    for c in outs:
        c.start()

    @pl.loop(0, NJB)
    def _(j):
        here = pl.ds(j * TILE, TILE)
        jbf[:, here, :] = jacc[:, here, :].astype(jnp.bfloat16)

    c = pltpu.make_async_copy(jbf, jobs_out, osems.at[2])
    c.start()
    c.wait()
    for c in outs:
        c.wait()


def sparse_products(meta, table, workers, tiles):
    hbm = pl.BlockSpec(memory_space=pl.ANY)
    flops = 2 * 2 * 2 * NB * TILE * TILE * 256
    return pl.pallas_call(
        sparse_kernel,
        grid_spec=pltpu.PrefetchScalarGridSpec(
            num_scalar_prefetch=1,
            grid=(),
            in_specs=[hbm] * 3,
            out_specs=[hbm] * 3,
            scratch_shapes=[
                pltpu.VMEM((2, NJ, TILE), jnp.bfloat16),
                pltpu.VMEM((2, NW_LOC, TILE), jnp.bfloat16),
                pltpu.VMEM((2 * NB, TILE, TILE), jnp.bfloat16),
                pltpu.VMEM((2, NJ, TILE), jnp.float32),
                pltpu.VMEM((2, NW_LOC, TILE), jnp.float32),
                pltpu.VMEM((2, NJ, TILE), jnp.bfloat16),
                pltpu.VMEM((NW_LOC, TILE), jnp.bfloat16),
                pltpu.SemaphoreType.DMA((2,)),
                pltpu.SemaphoreType.DMA((2 * NB // KCHUNK,)),
                pltpu.SemaphoreType.DMA((3,)),
            ],
        ),
        out_shape=[
            jax.ShapeDtypeStruct((2, NJ, TILE), jnp.bfloat16),
            jax.ShapeDtypeStruct((NW_LOC, TILE), jnp.bfloat16),
            jax.ShapeDtypeStruct((NW_LOC, TILE), jnp.float32),
        ],
        compiler_params=pltpu.CompilerParams(vmem_limit_bytes=56 * 2**20),
        cost_estimate=pl.CostEstimate(flops=flops, bytes_accessed=22 * 2**20, transcendentals=0),
        name="sparse_products",
    )(meta, table, workers, tiles)


def scatter_kernel(
    jobs,
    away,
    home,
    jout,
    wout,
    own0,
    own1,
    own2,
    ra0,
    ra1,
    ra2,
    sa0,
    sa1,
    sa2,
    rb0,
    rb1,
    rb2,
    sb0,
    sb1,
    sb2,
    rc0,
    rc1,
    rc2,
    rw,
    lsem,
    wsend,
    wrecv,
    gsend,
    grecv,
):
    own, ra, sa = (own0, own1, own2), (ra0, ra1, ra2), (sa0, sa1, sa2)
    rb, sb, rc = (rb0, rb1, rb2), (sb0, sb1, sb2), (rc0, rc1, rc2)
    at = position()
    x_lo = at["x"] % 2

    def rows(p):
        return pl.ds(PARTS[p][0], PARTS[p][1])

    def remote(src, dst, i, target):
        c = pltpu.make_async_remote_copy(
            src_ref=src,
            dst_ref=dst,
            send_sem=gsend.at[i],
            recv_sem=grecv.at[i],
            device_id=device(target),
            device_id_type=MESH,
        )
        c.start()
        return c

    local = []
    for p in range(3):
        a1 = PARTS[p][2][0]
        c = pltpu.make_async_copy(
            jobs.at[pick("xyz", {a1: at[a1]}) + (rows(p), slice(None))], own[p], lsem.at[p]
        )
        c.start()
        local.append(c)
    greet(at)
    first, second, third = {}, {}, {}
    for d in (2, 1, 3):
        for p in range(3):
            a1 = PARTS[p][2][0]
            target = shifted(at, a1, d)
            first[p, d] = remote(
                jobs.at[pick("xyz", {a1: target[a1]}) + (rows(p), slice(None))],
                ra[p].at[d - 1],
                p * 9 + d - 1,
                target,
            )
    partner = {**at, "x": at["x"] + 1 - 2 * x_lo}
    wcopy = pltpu.make_async_remote_copy(
        src_ref=away,
        dst_ref=rw,
        send_sem=wsend,
        recv_sem=wrecv,
        device_id=device(partner),
        device_id_type=MESH,
    )
    wcopy.start()

    def loop_index(axes, k):
        index = []
        for n in reversed(dims_of(axes)):
            index.append(k % n)
            k = k // n
        return tuple(reversed(index))

    for p in range(3):
        a1, a2, a3 = PARTS[p][2]
        local[p].wait()
        for d in (1, 2, 3):
            first[p, d].wait_recv()
        rest = "".join(a for a in "xyz" if a != a1)

        @pl.loop(0, 16)
        def _(k):
            i = loop_index(rest, k)
            total = own[p][i].astype(jnp.float32)
            for d in range(3):
                total += ra[p][(d,) + i].astype(jnp.float32)
            sa[p][i] = total

        for d in (2, 1, 3):
            target = shifted(at, a2, d)
            second[p, d] = remote(
                sa[p].at[pick(rest, {a2: target[a2]})], rb[p].at[d - 1], p * 9 + 3 + d - 1, target
            )
    for p in range(3):
        a1, a2, a3 = PARTS[p][2]
        rest = "".join(a for a in "xyz" if a != a1)
        for d in (1, 2, 3):
            second[p, d].wait_recv()

        @pl.loop(0, 4)
        def _(k):
            i = loop_index(a3, k)
            coordinate = i[0] if len(i) == 1 else i[1] * 2 + i[0]
            total = sa[p][pick(rest, {a2: at[a2], a3: coordinate})]
            for d in range(3):
                total += rb[p][(d,) + i]
            sb[p][i] = total

        for d in (2, 1, 3):
            target = shifted(at, a3, d)
            third[p, d] = remote(
                sb[p].at[pick(a3, {a3: target[a3]})], rc[p].at[d - 1], p * 9 + 6 + d - 1, target
            )
    wcopy.wait()

    @pl.loop(0, RB)
    def _(j):
        here = pl.ds(j * TILE, TILE)
        wout[here, :] = home[here, :] + rw[here, :].astype(jnp.float32)

    for p in range(3):
        a1, a2, a3 = PARTS[p][2]
        for d in (1, 2, 3):
            third[p, d].wait_recv()
        total = sb[p][pick(a3, {a3: at[a3]})]
        for d in range(3):
            total += rc[p][d]
        jout[rows(p), :] = total
    for c in list(first.values()) + list(second.values()) + list(third.values()):
        c.wait_send()


def scatter(jobs, away, home):
    hbm = pl.BlockSpec(memory_space=pl.ANY)
    vmem = pl.BlockSpec(memory_space=pltpu.VMEM)
    own, ra, sa, rb, sb, rc = [], [], [], [], [], []
    for _, n, (a1, a2, a3) in PARTS:
        after = dims_of("".join(a for a in "xyz" if a != a1)) + (n, TILE)
        last = dims_of(a3) + (n, TILE)
        own.append(pltpu.VMEM(after, jnp.bfloat16))
        ra.append(pltpu.VMEM((3,) + after, jnp.bfloat16))
        sa.append(pltpu.VMEM(after, jnp.float32))
        rb.append(pltpu.VMEM((3,) + last, jnp.float32))
        sb.append(pltpu.VMEM(last, jnp.float32))
        rc.append(pltpu.VMEM((3, n, TILE), jnp.float32))
    return pl.pallas_call(
        scatter_kernel,
        in_specs=[hbm, hbm, vmem],
        out_specs=[vmem, vmem],
        out_shape=[
            jax.ShapeDtypeStruct((JLOC, TILE), jnp.float32),
            jax.ShapeDtypeStruct((NW_LOC, TILE), jnp.float32),
        ],
        scratch_shapes=own
        + ra
        + sa
        + rb
        + sb
        + rc
        + [
            pltpu.VMEM((NW_LOC, TILE), jnp.bfloat16),
            pltpu.SemaphoreType.DMA((3,)),
            pltpu.SemaphoreType.DMA,
            pltpu.SemaphoreType.DMA,
            pltpu.SemaphoreType.DMA((27,)),
            pltpu.SemaphoreType.DMA((27,)),
        ],
        compiler_params=pltpu.CompilerParams(
            collective_id=1, has_side_effects=True, vmem_limit_bytes=56 * 2**20
        ),
        name="scatter_sums",
    )(jobs, away, home)


def on_device(
    worker_emb,
    job_emb,
    worker_cot,
    job_cot,
    worker_deg,
    job_deg,
    block_rows,
    block_cols,
    block_tiles,
    live_count,
):
    quarter = worker_emb.shape[1]
    worker_scale = lax.rsqrt(worker_deg.astype(jnp.float32))[:, None]
    job_scale = lax.rsqrt(job_deg.astype(jnp.float32))[:, None]
    worker_src = jnp.concatenate(
        [worker_emb * worker_scale, worker_cot * worker_scale], axis=1
    ).astype(jnp.bfloat16)
    job_src = jnp.concatenate([job_emb * job_scale, job_cot * job_scale], axis=1).astype(
        jnp.bfloat16
    )
    live = jnp.broadcast_to(live_count[0, 0], (NB,))
    x_lo = jnp.broadcast_to((lax.axis_index("col") // 2).astype(jnp.int32), (NB,))
    zero = jnp.zeros((NB,), jnp.int32)
    meta = jnp.stack([block_rows, block_cols, live, x_lo, zero, zero, zero, zero])
    table, workers, tiles, metas = gather(worker_src, job_src, block_tiles, meta)
    jobs, away, home = sparse_products(
        metas,
        table.reshape(2, NJ, TILE),
        workers,
        tiles.reshape(2 * NB, TILE, TILE),
    )
    job_part, worker_part = scatter(jobs.reshape(dims_of("xyz") + (JLOC, TILE)), away, home)
    worker_out = worker_scale * worker_part[:, :quarter]
    worker_grad = worker_scale * worker_part[:, quarter:]
    job_out = job_scale * job_part[:, :quarter]
    job_grad = job_scale * job_part[:, quarter:]
    return (worker_out, job_out, worker_grad, job_grad)


def solution(mesh):
    return jax.shard_map(
        on_device,
        mesh=mesh,
        in_specs=(
            P("blk", "col"),
            P("blk", "col"),
            P("blk", "col"),
            P("blk", "col"),
            P("blk"),
            P("blk"),
            P(("blk", "col")),
            P(("blk", "col")),
            P(("blk", "col"), None, None),
            P("blk", "col"),
        ),
        out_specs=(P("blk", "col"), P("blk", "col"), P("blk", "col"), P("blk", "col")),
        check_vma=False,
    )
```

```python
import jax
import jax.numpy as jnp
from jax import lax
from jax.experimental import pallas as pl
from jax.experimental.pallas import tpu as pltpu
from jax.sharding import PartitionSpec as P

MESH = pl.DeviceIdType.MESH
TILE = 128
NB = 128
RB = 16
NJB = 64
NW_LOC = RB * TILE
NJ = NJB * TILE
JLOC = 256
PARTS = ((0, 32, "xyz"), (32, 48, "yzx"), (80, 48, "zxy"))
DIMS = (("x", 2), ("z", 4), ("x", 2), ("y", 4))
TCHUNK = 8
NCHUNK = NB // TCHUNK
NBUF = 4
GROUP = 16
SLOTS = 2 * NB


def position():
    blk = lax.axis_index("blk")
    col = lax.axis_index("col")
    return {
        "z": blk // 8,
        "x": ((blk // 4) % 2) * 2 + col // 2,
        "y": blk % 4,
        "core": col % 2,
    }


def device(at):
    x = at["x"]
    return (at["z"] * 8 + (x // 2) * 4 + at["y"], (x % 2) * 2 + at["core"])


def shifted(at, axis, by):
    return {**at, axis: (at[axis] + by + 4) % 4}


def neighbours(at):
    out = [device(shifted(at, axis, d)) for axis in "xyz" for d in (1, 2, 3)]
    out.append(device({**at, "core": 1 - at["core"]}))
    return out


def dims_of(axes):
    return tuple(n for name, n in DIMS if name in axes)


def pick(axes, fixed):
    index = []
    seen_x = False
    for name, _ in DIMS:
        if name not in axes:
            continue
        if name not in fixed:
            index.append(slice(None))
        elif name == "x":
            index.append(fixed["x"] // 2 if seen_x else fixed["x"] % 2)
        else:
            index.append(fixed[name])
        if name == "x":
            seen_x = True
    return tuple(index)


def part_rows(p):
    return pl.ds(PARTS[p][0], PARTS[p][1])


def chunk_part(ref, p, fixed):
    return ref.at[pick("xyz", fixed) + (slice(None), part_rows(p), slice(None))]


def loop_index(axes, k):
    index = []
    for n in reversed(dims_of(axes)):
        index.append(k % n)
        k = k // n
    return tuple(reversed(index))


def block_index(j):
    return (j >> 4, (j >> 3) & 1, (j >> 1) & 3, j & 1)


def order_slots(meta, table):
    lane = lax.broadcasted_iota(jnp.int32, (1, NB), 1)
    place = lax.broadcasted_iota(jnp.int32, (NB, SLOTS), 1)
    block = lax.broadcasted_iota(jnp.int32, (NB, NB), 1)

    def column(row):
        return jnp.transpose(jnp.broadcast_to(row, (NB, NB)))

    def count_down(flags):
        return jnp.sum(jnp.where(flags, 1, 0), axis=0, keepdims=True)

    payloads, cols, rows = [], [], []
    for h in range(2):
        ok = lane < meta[h, 2:3, :]
        r, c = meta[h, 0:1, :], meta[h, 1:2, :]
        payloads.append(lane + h * NB + r * SLOTS + c * (SLOTS * RB))
        cols.append(jnp.where(ok, c, NJB))
        rows.append(jnp.where(ok, r, RB))
    for line, (keys, at) in enumerate(((cols, 2), (rows, 4))):
        unique = [keys[h] * SLOTS + lane + h * NB for h in range(2)]
        across = jnp.broadcast_to(jnp.concatenate(unique, axis=1), (NB, SLOTS))
        rank = jnp.zeros((1, SLOTS), jnp.int32)
        for h in range(2):
            down = column(unique[h])
            rank += count_down(jnp.concatenate([down, down], axis=1) < across)
        ordered = jnp.zeros((1, SLOTS), jnp.int32)
        upto = jnp.zeros((1, NB), jnp.int32)
        count = jnp.zeros((1, NB), jnp.int32)
        for h in range(2):
            spot = column(rank[:, h * NB : (h + 1) * NB])
            hit = place == jnp.concatenate([spot, spot], axis=1)
            value = column(payloads[h])
            value = jnp.concatenate([value, value], axis=1)
            ordered += jnp.sum(jnp.where(hit, value, 0), axis=0, keepdims=True)
            key = column(keys[h])
            upto += count_down(key <= block)
            count += count_down(key == block)
        table[line : line + 1, :] = ordered
        table[at : at + 1, :NB] = jnp.maximum(upto - 1, 0)
        table[at + 1 : at + 2, :NB] = count


def layer_kernel(
    wemb,
    wcot,
    jemb,
    jcot,
    wdeg,
    jdeg,
    brows,
    bcols,
    live,
    tiles,
    wsum,
    jsum,
    wbuf,
    dense_in,
    tin,
    xbuf,
    table,
    rows_in,
    meta,
    order,
    slots,
    cbuf,
    jobs,
    away,
    home,
    rw,
    ra0,
    ra1,
    ra2,
    sa0,
    sa1,
    sa2,
    rb0,
    rb1,
    rb2,
    sb0,
    sb1,
    sb2,
    rc0,
    rc1,
    rc2,
    in_sem,
    tin_sem,
    tsend,
    trecv,
    osend,
    orecv,
    gsend,
    grecv,
    ssend,
    srecv,
):
    ra, sa = (ra0, ra1, ra2), (sa0, sa1, sa2)
    rb, sb, rc = (rb0, rb1, rb2), (sb0, sb1, sb2), (rc0, rc1, rc2)
    at = position()
    x_lo = at["x"] % 2
    core = at["core"]
    core_mate = {**at, "core": 1 - core}
    x_mate = {**at, "x": at["x"] + 1 - 2 * x_lo}
    f32, bf16 = jnp.float32, jnp.bfloat16

    def load(i):
        return pltpu.make_async_copy(
            tiles.at[pl.ds(i * TCHUNK, TCHUNK)], tin.at[i % NBUF], tin_sem.at[i % NBUF]
        )

    def remote(src, dst, sems, rems, i, target):
        c = pltpu.make_async_remote_copy(
            src_ref=src,
            dst_ref=dst,
            send_sem=sems.at[i],
            recv_sem=rems.at[i],
            device_id=device(target),
            device_id_type=MESH,
        )
        c.start()
        return c

    barrier = pltpu.get_barrier_semaphore()
    others = neighbours(at)
    for other in others:
        pl.semaphore_signal(barrier, inc=1, device_id=other, device_id_type=MESH)
    ins = [
        pltpu.make_async_copy(jemb, rows_in.at[pl.ds(0, 64)], in_sem.at[0]),
        pltpu.make_async_copy(jcot, rows_in.at[pl.ds(64, 64)], in_sem.at[1]),
        pltpu.make_async_copy(wemb, dense_in.at[pl.ds(0, 64)], in_sem.at[2]),
        pltpu.make_async_copy(wcot, dense_in.at[pl.ds(64, 64)], in_sem.at[3]),
    ]
    for c in ins:
        c.start()
    for i in range(NBUF):
        load(i).start()

    job_scale = lax.rsqrt(jdeg[...].astype(f32))
    worker_scale = lax.rsqrt(wdeg[...].astype(f32))
    meta[core] = jnp.zeros((8, NB), jnp.int32)
    order[...] = jnp.zeros((8, SLOTS), jnp.int32)
    meta[core, 0:1, :] = brows[...]
    meta[core, 1:2, :] = bcols[...]
    meta[core, 2:3, :] = jnp.broadcast_to(live[...], (1, NB))
    ins[0].wait()
    ins[1].wait()
    for i in range(2):
        here = slice(i * TILE, (i + 1) * TILE)
        table[pick("xyz", at) + (i,)] = jnp.transpose(
            rows_in[:, here] * job_scale[:, here]
        ).astype(bf16)
    pl.semaphore_wait(barrier, len(others))
    first, second, third = {}, {}, {}
    for d in (1, 3, 2):
        for p in range(3):
            own = chunk_part(table, p, at)
            first[p, d] = remote(
                own, own, gsend, grecv, p * 18 + d - 1, shifted(at, PARTS[p][2][0], d)
            )
    mcopy = remote(meta.at[core], meta.at[core], osend, orecv, 0, core_mate)
    ins[2].wait()
    ins[3].wait()
    for i in range(RB):
        here = slice(i * TILE, (i + 1) * TILE)
        wbuf[x_lo, i] = jnp.transpose(dense_in[:, here] * worker_scale[:, here]).astype(bf16)
    wcopy = remote(wbuf.at[x_lo], wbuf.at[x_lo], osend, orecv, 1, x_mate)

    tcopies = []

    def chunk(i):
        load(i).wait()
        here = pl.ds(core * NB + i * TCHUNK, TCHUNK)
        xbuf[here] = tin[i % NBUF].astype(f32).astype(bf16)
        if i + NBUF < NCHUNK:
            load(i + NBUF).start()
        tcopies.append(remote(xbuf.at[here], xbuf.at[here], tsend, trecv, i, core_mate))

    for i in range(NCHUNK // 2):
        chunk(i)
    for p in range(3):
        a1, a2, a3 = PARTS[p][2]
        for d in (1, 2, 3):
            first[p, d].wait_recv()
        own = chunk_part(table, p, {a2: at[a2], a3: at[a3]})
        for d in (1, 3, 2):
            second[p, d] = remote(own, own, gsend, grecv, p * 18 + 3 + d - 1, shifted(at, a2, d))
    for p in range(3):
        a1, a2, a3 = PARTS[p][2]
        own = chunk_part(table, p, {a2: at[a2], a3: at[a3]})
        for d in (1, 3, 2):
            third[p, 0, d] = remote(own, own, gsend, grecv, p * 18 + 6 + d - 1, shifted(at, a3, d))
    for i in range(NCHUNK // 2, NCHUNK):
        chunk(i)
    for g in (1, 3, 2):
        for p in range(3):
            a1, a2, a3 = PARTS[p][2]
            second[p, g].wait_recv()
            got = chunk_part(table, p, {a2: (at[a2] - g + 4) % 4, a3: at[a3]})
            for d in (1, 3, 2):
                third[p, g, d] = remote(
                    got, got, gsend, grecv, p * 18 + 6 + g * 3 + d - 1, shifted(at, a3, d)
                )
    mcopy.wait()
    order_slots(meta, order)
    to_scalars = pltpu.make_async_copy(order, slots, in_sem.at[0])
    to_scalars.start()
    to_scalars.wait()
    for c in tcopies:
        c.wait_recv()
    wcopy.wait()

    def running(line, product, key):
        def step(q, total):
            for g in range(GROUP):
                k = q * GROUP + g
                entry = slots[line, k]
                before = slots[line, jnp.maximum(k - 1, 0)]
                fresh = key(entry) != key(before)
                total = jnp.where(fresh, 0.0, total) + product(
                    entry & (SLOTS - 1), (entry >> 8) & (RB - 1), (entry >> 12) & (NJB - 1)
                )
                cbuf[k, 0] = total[:, :TILE].astype(bf16)
                cbuf[k, 1] = total[:, TILE:].astype(bf16)
            return total

        lax.fori_loop(0, SLOTS // GROUP, step, jnp.zeros((TILE, 2 * TILE), f32))

    def to_jobs(s, r, c):
        workers = jnp.concatenate([wbuf[0, r], wbuf[1, r]], axis=1)
        return lax.dot_general(
            xbuf[s], workers, (((0,), (0,)), ((), ())), preferred_element_type=f32
        )

    def to_workers(s, r, c):
        i = block_index(c)
        rows = jnp.concatenate([table[(0,) + i], table[(1,) + i]], axis=1)
        return jnp.dot(xbuf[s], rows, preferred_element_type=f32)

    running(0, to_jobs, lambda entry: entry >> 12)

    @pl.loop(0, NJB)
    def _(j):
        last = slots[2, j] & (SLOTS - 1)
        some = slots[3, j] > 0
        for half in range(2):
            value = cbuf[last, half]
            jobs[(half,) + block_index(j)] = jnp.where(some, value, jnp.zeros_like(value))

    sfirst, ssecond, sthird = {}, {}, {}
    for d in (2, 1, 3):
        for p in range(3):
            a1 = PARTS[p][2][0]
            target = shifted(at, a1, d)
            sfirst[p, d] = remote(
                chunk_part(jobs, p, {a1: target[a1]}),
                ra[p].at[d - 1],
                ssend,
                srecv,
                p * 9 + d - 1,
                target,
            )
    for c in third.values():
        c.wait_recv()
    running(1, to_workers, lambda entry: (entry >> 8) & (RB - 1))

    @pl.loop(0, RB)
    def _(j):
        last = slots[4, j] & (SLOTS - 1)
        some = slots[5, j] > 0
        for ref, half in ((away, 1 - x_lo), (home, x_lo)):
            value = cbuf[last, half]
            ref[j] = jnp.where(some, value, jnp.zeros_like(value))

    acopy = remote(away, rw, osend, orecv, 2, x_mate)

    for p in range(3):
        a1, a2, a3 = PARTS[p][2]
        for d in (1, 2, 3):
            sfirst[p, d].wait_recv()
        rest = "".join(a for a in "xyz" if a != a1)
        rows = part_rows(p)

        @pl.loop(0, 16)
        def _(k):
            i = loop_index(rest, k)
            others = iter(i)
            mine = iter((at["x"] % 2, at["x"] // 2) if a1 == "x" else (at[a1],))
            here = tuple(next(mine) if name == a1 else next(others) for name, _ in DIMS)
            total = jobs[here + (slice(None), rows, slice(None))].astype(f32)
            for d in range(3):
                total += ra[p][(d,) + i].astype(f32)
            sa[p][i] = total

        for d in (2, 1, 3):
            target = shifted(at, a2, d)
            ssecond[p, d] = remote(
                sa[p].at[pick(rest, {a2: target[a2]})],
                rb[p].at[d - 1],
                ssend,
                srecv,
                p * 9 + 3 + d - 1,
                target,
            )
    for p in range(3):
        a1, a2, a3 = PARTS[p][2]
        rest = "".join(a for a in "xyz" if a != a1)
        for d in (1, 2, 3):
            ssecond[p, d].wait_recv()

        @pl.loop(0, 4)
        def _(k):
            i = loop_index(a3, k)
            coordinate = i[0] if len(i) == 1 else i[1] * 2 + i[0]
            total = sa[p][pick(rest, {a2: at[a2], a3: coordinate})]
            for d in range(3):
                total += rb[p][(d,) + i]
            sb[p][i] = total

        for d in (2, 1, 3):
            target = shifted(at, a3, d)
            sthird[p, d] = remote(
                sb[p].at[pick(a3, {a3: target[a3]})],
                rc[p].at[d - 1],
                ssend,
                srecv,
                p * 9 + 6 + d - 1,
                target,
            )
    acopy.wait()
    for i in range(RB):
        here = slice(i * TILE, (i + 1) * TILE)
        wsum[here, :] = home[i].astype(f32) + rw[i].astype(f32)
    for p in range(3):
        a1, a2, a3 = PARTS[p][2]
        for d in (1, 2, 3):
            sthird[p, d].wait_recv()
        total = sb[p][pick(a3, {a3: at[a3]})]
        for d in range(3):
            total += rc[p][d]
        jsum[:, part_rows(p), :] = total
    for copies in (first, second, third, sfirst, ssecond, sthird):
        for c in copies.values():
            c.wait_send()
    for c in tcopies:
        c.wait_send()


def layer(wemb, wcot, jemb, jcot, wdeg, jdeg, brows, bcols, live, tiles):
    hbm = pl.BlockSpec(memory_space=pl.ANY)
    vmem = pl.BlockSpec(memory_space=pltpu.VMEM)
    ra, sa, rb, sb, rc = [], [], [], [], []
    for _, n, (a1, a2, a3) in PARTS:
        after = dims_of("".join(a for a in "xyz" if a != a1)) + (2, n, TILE)
        last = dims_of(a3) + (2, n, TILE)
        ra.append(pltpu.VMEM((3,) + after, jnp.bfloat16))
        sa.append(pltpu.VMEM(after, jnp.float32))
        rb.append(pltpu.VMEM((3,) + last, jnp.float32))
        sb.append(pltpu.VMEM(last, jnp.float32))
        rc.append(pltpu.VMEM((3, 2, n, TILE), jnp.float32))
    chunks = dims_of("xyz") + (2, TILE, TILE)
    dma = pltpu.SemaphoreType.DMA
    return pl.pallas_call(
        layer_kernel,
        in_specs=[hbm] * 4 + [vmem] * 5 + [hbm],
        out_specs=[vmem] * 2,
        out_shape=[
            jax.ShapeDtypeStruct((NW_LOC, TILE), jnp.float32),
            jax.ShapeDtypeStruct((2, TILE, TILE), jnp.float32),
        ],
        scratch_shapes=[
            pltpu.VMEM((2, RB, TILE, TILE), jnp.bfloat16),
            pltpu.VMEM((TILE, NW_LOC), jnp.float32),
            pltpu.VMEM((NBUF, TCHUNK, TILE, TILE), jnp.int32),
            pltpu.VMEM((SLOTS, TILE, TILE), jnp.bfloat16),
            pltpu.VMEM(chunks, jnp.bfloat16),
            pltpu.VMEM((TILE, JLOC), jnp.float32),
            pltpu.VMEM((2, 8, NB), jnp.int32),
            pltpu.VMEM((8, SLOTS), jnp.int32),
            pltpu.SMEM((8, SLOTS), jnp.int32),
            pltpu.VMEM((SLOTS, 2, TILE, TILE), jnp.bfloat16),
            pltpu.VMEM(chunks, jnp.bfloat16),
            pltpu.VMEM((RB, TILE, TILE), jnp.bfloat16),
            pltpu.VMEM((RB, TILE, TILE), jnp.bfloat16),
            pltpu.VMEM((RB, TILE, TILE), jnp.bfloat16),
        ]
        + ra
        + sa
        + rb
        + sb
        + rc
        + [
            dma((4,)),
            dma((NBUF,)),
            dma((NCHUNK,)),
            dma((NCHUNK,)),
            dma((3,)),
            dma((3,)),
            dma((54,)),
            dma((54,)),
            dma((27,)),
            dma((27,)),
        ],
        compiler_params=pltpu.CompilerParams(
            collective_id=0, has_side_effects=True, vmem_limit_bytes=60 * 2**20
        ),
        name="layer",
    )(wemb, wcot, jemb, jcot, wdeg, jdeg, brows, bcols, live, tiles)


def finish_kernel(wsum, jsum, wdeg, jdeg, wout, wgrad, jout, jgrad):
    for total, deg, out, grad in ((wsum, wdeg, wout, wgrad), (jsum, jdeg, jout, jgrad)):
        scale = lax.rsqrt(deg[...].astype(jnp.float32))
        for i in range(total.shape[0] // TILE):
            here = slice(i * TILE, (i + 1) * TILE)
            value = jnp.transpose(total[here, :]) * scale[:, here]
            out[:, here] = value[:64]
            grad[:, here] = value[64:]


def finish(wsum, jsum, wdeg, jdeg):
    vmem = pl.BlockSpec(memory_space=pltpu.VMEM)
    return pl.pallas_call(
        finish_kernel,
        in_specs=[vmem] * 4,
        out_specs=[vmem] * 4,
        out_shape=[
            jax.ShapeDtypeStruct((64, NW_LOC), jnp.float32),
            jax.ShapeDtypeStruct((64, NW_LOC), jnp.float32),
            jax.ShapeDtypeStruct((64, JLOC), jnp.float32),
            jax.ShapeDtypeStruct((64, JLOC), jnp.float32),
        ],
        name="finish",
    )(wsum, jsum, wdeg, jdeg)


def on_device(
    worker_emb,
    job_emb,
    worker_cot,
    job_cot,
    worker_deg,
    job_deg,
    block_rows,
    block_cols,
    block_tiles,
    live_count,
):
    wdeg, jdeg = worker_deg[None, :], job_deg[None, :]
    wsum, jsum = layer(
        worker_emb.T,
        worker_cot.T,
        job_emb.T,
        job_cot.T,
        wdeg,
        jdeg,
        block_rows[None, :],
        block_cols[None, :],
        live_count,
        block_tiles,
    )
    worker_out, worker_grad, job_out, job_grad = finish(wsum, jsum.reshape(JLOC, TILE), wdeg, jdeg)
    return (worker_out.T, job_out.T, worker_grad.T, job_grad.T)


def solution(mesh):
    return jax.shard_map(
        on_device,
        mesh=mesh,
        in_specs=(
            P("blk", "col"),
            P("blk", "col"),
            P("blk", "col"),
            P("blk", "col"),
            P("blk"),
            P("blk"),
            P(("blk", "col")),
            P(("blk", "col")),
            P(("blk", "col"), None, None),
            P("blk", "col"),
        ),
        out_specs=(P("blk", "col"), P("blk", "col"), P("blk", "col"), P("blk", "col")),
        check_vma=False,
    )
```

```python
import jax
import jax.numpy as jnp
from jax import lax
from jax.experimental import pallas as pl
from jax.experimental.pallas import tpu as pltpu
from jax.sharding import PartitionSpec as P

MESH = pl.DeviceIdType.MESH
TILE = 128
NB = 128
RB = 16
NJB = 64
NW_LOC = RB * TILE
NJ = NJB * TILE
JLOC = 256
SPREAD = ((0, 48, "xyz"), (48, 48, "xzy"), (96, 32, "yzx"))
REDUCE = (
    (0, 48, "yzx", 0),
    (48, 48, "zyx", 0),
    (0, 48, "yzx", 1),
    (48, 48, "zyx", 1),
    (96, 32, "xyz", None),
)
LABELS = {"x_lo": 2, "z": 4, "x_hi": 2, "y": 4}
DIMS = (("x", 2), ("z", 4), ("x", 2), ("y", 4))
TCHUNK = 8
NCHUNK = NB // TCHUNK
NBUF = 4
GROUP = 16
SLOTS = 2 * NB


def position():
    blk = lax.axis_index("blk")
    col = lax.axis_index("col")
    return {
        "z": blk // 8,
        "x": ((blk // 4) % 2) * 2 + col // 2,
        "y": blk % 4,
        "core": col % 2,
    }


def device(at):
    x = at["x"]
    return (at["z"] * 8 + (x // 2) * 4 + at["y"], (x % 2) * 2 + at["core"])


def shifted(at, axis, by):
    return {**at, axis: (at[axis] + by + 4) % 4}


def neighbours(at):
    out = [device(shifted(at, axis, d)) for axis in "xyz" for d in (1, 2, 3)]
    out.append(device({**at, "core": 1 - at["core"]}))
    return out


def dims_of(axes):
    return tuple(n for name, n in DIMS if name in axes)


def pick(axes, fixed):
    index = []
    seen_x = False
    for name, _ in DIMS:
        if name not in axes:
            continue
        if name not in fixed:
            index.append(slice(None))
        elif name == "x":
            index.append(fixed["x"] // 2 if seen_x else fixed["x"] % 2)
        else:
            index.append(fixed[name])
        if name == "x":
            seen_x = True
    return tuple(index)


def part_rows(part):
    return pl.ds(part[0], part[1])


def chunk_part(ref, part, fixed):
    return ref.at[pick("xyz", fixed) + (slice(None), part_rows(part), slice(None))]


def labels_of(axis, coordinate):
    return {"x_lo": coordinate % 2, "x_hi": coordinate // 2} if axis == "x" else {axis: coordinate}


def plan(part):
    _, _, (a1, a2, _), wave = part
    after = [x for x in LABELS if x not in labels_of(a1, 0) and (wave is None or x != "x_lo")]
    return after, [x for x in after if x not in labels_of(a2, 0)]


def index(labels, fixed):
    return tuple(fixed.get(x, slice(None)) for x in labels)


def loop_labels(labels, k):
    fixed = {}
    for x in reversed(labels):
        fixed[x] = k % LABELS[x]
        k = k // LABELS[x]
    return fixed


def block_index(j):
    return (j >> 4, (j >> 3) & 1, (j >> 1) & 3, j & 1)


def order_slots(meta, table):
    lane = lax.broadcasted_iota(jnp.int32, (1, NB), 1)
    place = lax.broadcasted_iota(jnp.int32, (NB, SLOTS), 1)
    block = lax.broadcasted_iota(jnp.int32, (NB, NB), 1)

    def column(row):
        return jnp.transpose(jnp.broadcast_to(row, (NB, NB)))

    def count_down(flags):
        return jnp.sum(jnp.where(flags, 1, 0), axis=0, keepdims=True)

    payloads, cols, rows = [], [], []
    for h in range(2):
        ok = lane < meta[h, 2:3, :]
        r, c = meta[h, 0:1, :], meta[h, 1:2, :]
        payloads.append(lane + h * NB + r * SLOTS + c * (SLOTS * RB))
        cols.append(jnp.where(ok, c, NJB))
        rows.append(jnp.where(ok, r, RB))
    for line, (keys, at) in enumerate(((cols, 2), (rows, 4))):
        unique = [keys[h] * SLOTS + lane + h * NB for h in range(2)]
        across = jnp.broadcast_to(jnp.concatenate(unique, axis=1), (NB, SLOTS))
        rank = jnp.zeros((1, SLOTS), jnp.int32)
        for h in range(2):
            down = column(unique[h])
            rank += count_down(jnp.concatenate([down, down], axis=1) < across)
        ordered = jnp.zeros((1, SLOTS), jnp.int32)
        upto = jnp.zeros((1, NB), jnp.int32)
        count = jnp.zeros((1, NB), jnp.int32)
        for h in range(2):
            spot = column(rank[:, h * NB : (h + 1) * NB])
            hit = place == jnp.concatenate([spot, spot], axis=1)
            value = column(payloads[h])
            value = jnp.concatenate([value, value], axis=1)
            ordered += jnp.sum(jnp.where(hit, value, 0), axis=0, keepdims=True)
            key = column(keys[h])
            upto += count_down(key <= block)
            count += count_down(key == block)
        table[line : line + 1, :] = ordered
        table[at : at + 1, :NB] = jnp.maximum(upto - 1, 0)
        table[at + 1 : at + 2, :NB] = count


def layer_kernel(
    wemb,
    wcot,
    jemb,
    jcot,
    wdeg,
    jdeg,
    brows,
    bcols,
    live,
    tiles,
    home,
    rw,
    jsum,
    wown,
    wother,
    dense_in,
    tin,
    xbuf,
    table,
    rows_in,
    meta,
    order,
    slots,
    cbuf,
    jobs,
    away,
    kept,
    *rest,
):
    ra, sa, rb, sb, rc = (rest[i : i + len(REDUCE)] for i in range(0, 5 * len(REDUCE), len(REDUCE)))
    in_sem, tin_sem, tsend, trecv, osend, orecv, gsend, grecv, ssend, srecv = rest[5 * len(REDUCE) :]
    at = position()
    x_lo = at["x"] % 2
    core = at["core"]
    core_mate = {**at, "core": 1 - core}
    x_mate = {**at, "x": at["x"] + 1 - 2 * x_lo}
    f32, bf16 = jnp.float32, jnp.bfloat16

    def load(i):
        return pltpu.make_async_copy(
            tiles.at[pl.ds(i * TCHUNK, TCHUNK)], tin.at[i % NBUF], tin_sem.at[i % NBUF]
        )

    def remote(src, dst, sems, rems, i, target):
        c = pltpu.make_async_remote_copy(
            src_ref=src,
            dst_ref=dst,
            send_sem=sems.at[i],
            recv_sem=rems.at[i],
            device_id=device(target),
            device_id_type=MESH,
        )
        c.start()
        return c

    barrier = pltpu.get_barrier_semaphore()
    others = neighbours(at)
    for other in others:
        pl.semaphore_signal(barrier, inc=1, device_id=other, device_id_type=MESH)
    ins = [
        pltpu.make_async_copy(jemb, rows_in.at[pl.ds(0, 64)], in_sem.at[0]),
        pltpu.make_async_copy(jcot, rows_in.at[pl.ds(64, 64)], in_sem.at[1]),
        pltpu.make_async_copy(wemb, dense_in.at[pl.ds(0, 64)], in_sem.at[2]),
        pltpu.make_async_copy(wcot, dense_in.at[pl.ds(64, 64)], in_sem.at[3]),
    ]
    for c in ins:
        c.start()
    for i in range(NBUF):
        load(i).start()

    job_scale = lax.rsqrt(jdeg[...].astype(f32))
    worker_scale = lax.rsqrt(wdeg[...].astype(f32))
    meta[core] = jnp.zeros((8, NB), jnp.int32)
    order[...] = jnp.zeros((8, SLOTS), jnp.int32)
    meta[core, 0:1, :] = brows[...]
    meta[core, 1:2, :] = bcols[...]
    meta[core, 2:3, :] = jnp.broadcast_to(live[...], (1, NB))
    ins[0].wait()
    ins[1].wait()
    for i in range(2):
        here = slice(i * TILE, (i + 1) * TILE)
        table[pick("xyz", at) + (i,)] = jnp.transpose(
            rows_in[:, here] * job_scale[:, here]
        ).astype(bf16)
    pl.semaphore_wait(barrier, len(others))
    first, second, third = {}, {}, {}
    for d in (1, 3, 2):
        for p in range(3):
            own = chunk_part(table, SPREAD[p], at)
            first[p, d] = remote(
                own, own, gsend, grecv, p * 22 + d - 1, shifted(at, SPREAD[p][2][0], d)
            )
    mcopy = remote(meta.at[core], meta.at[core], osend, orecv, 0, core_mate)
    ins[2].wait()
    ins[3].wait()
    for i in range(RB):
        here = slice(i * TILE, (i + 1) * TILE)
        wown[i] = jnp.transpose(dense_in[:, here] * worker_scale[:, here]).astype(bf16)
    wcopy = remote(wown, wother, osend, orecv, 1, x_mate)

    tcopies = []

    def chunk(i):
        load(i).wait()
        here = pl.ds(core * NB + i * TCHUNK, TCHUNK)
        xbuf[here] = tin[i % NBUF].astype(f32).astype(bf16)
        if i + NBUF < NCHUNK:
            load(i + NBUF).start()
        tcopies.append(remote(xbuf.at[here], xbuf.at[here], tsend, trecv, i, core_mate))

    def spread(p, g):
        a1, a2, a3 = SPREAD[p][2]
        got = chunk_part(table, SPREAD[p], {a2: (at[a2] - g + 4) % 4, a3: at[a3]})
        for d in (1, 3, 2):
            third[p, g, d] = remote(
                got, got, gsend, grecv, p * 22 + 6 + g * 4 + d - 1, shifted(at, a3, d)
            )

    for p in range(3):
        a1, a2, a3 = SPREAD[p][2]
        for d in (1, 2, 3):
            first[p, d].wait_recv()
        own = chunk_part(table, SPREAD[p], {a2: at[a2], a3: at[a3]})
        for d in (1, 3, 2):
            second[p, d] = remote(own, own, gsend, grecv, p * 22 + 3 + d - 1, shifted(at, a2, d))
    for p in range(3):
        spread(p, 0)
    for i in range(NCHUNK // 2):
        chunk(i)
    for g in (1, 3, 2):
        for p in range(3):
            second[p, g].wait_recv()
            spread(p, g)
    for i in range(NCHUNK // 2, NCHUNK):
        chunk(i)
    mcopy.wait()
    order_slots(meta, order)
    to_scalars = pltpu.make_async_copy(order, slots, in_sem.at[0])
    to_scalars.start()
    to_scalars.wait()
    for c in tcopies:
        c.wait_recv()

    def running(line, product, key, total, start, stop, halves):
        def step(q, total):
            for g in range(GROUP):
                k = q * GROUP + g
                entry = slots[line, k]
                before = slots[line, jnp.maximum(k - 1, 0)]
                fresh = key(entry) != key(before)
                total = jnp.where(fresh, 0.0, total) + product(
                    entry & (SLOTS - 1), (entry >> 8) & (RB - 1), (entry >> 12) & (NJB - 1)
                )
                for i, half in enumerate(halves):
                    cbuf[k, half] = total[:, i * TILE : (i + 1) * TILE].astype(bf16)
            return total

        return lax.fori_loop(start // GROUP, stop // GROUP, step, total)

    def to_workers(s, r, c):
        i = block_index(c)
        rows = jnp.concatenate([table[(0,) + i], table[(1,) + i]], axis=1)
        return jnp.dot(xbuf[s], rows, preferred_element_type=f32)

    def sum_jobs(half, workers):
        def to_jobs(s, r, c):
            return lax.dot_general(
                xbuf[s], workers[r], (((0,), (0,)), ((), ())), preferred_element_type=f32
            )

        total = jnp.zeros((TILE, TILE), f32)
        running(0, to_jobs, lambda entry: entry >> 12, total, 0, SLOTS, (0,))

        @pl.loop(0, NJB, unroll=4)
        def _(j):
            last = slots[2, j] & (SLOTS - 1)
            some = slots[3, j] > 0
            value = cbuf[last, 0]
            jobs[(half,) + block_index(j)] = jnp.where(some, value, jnp.zeros_like(value))

    hops = {}
    wave_lo = (x_lo, 1 - x_lo)

    def hop(p, stage, d, src, dst):
        target = shifted(at, REDUCE[p][2][stage], d)
        hops[p, stage, d] = remote(src, dst, ssend, srecv, p * 9 + stage * 3 + d - 1, target)

    def fixed_of(p, axis, by):
        fixed = labels_of(axis, (at[axis] + by) % 4)
        if REDUCE[p][3] is not None and axis != "x":
            fixed["x_lo"] = wave_lo[REDUCE[p][3]]
        return fixed

    def first_hop(p):
        rows = (slice(None), part_rows(REDUCE[p]), slice(None))
        for d in (2, 1, 3):
            fixed = fixed_of(p, REDUCE[p][2][0], d)
            hop(p, 0, d, jobs.at[index(LABELS, fixed) + rows], ra[p].at[d - 1])

    def first_sum(p, fixed):
        own = {**fixed_of(p, REDUCE[p][2][0], 0), **fixed}
        rows = (slice(None), part_rows(REDUCE[p]), slice(None))
        total = jobs[index(LABELS, own) + rows].astype(f32)
        for d in range(3):
            total += ra[p][(d,) + index(plan(REDUCE[p])[0], fixed)].astype(f32)
        return total

    def second_hop(p):
        after, _ = plan(REDUCE[p])
        for d in (1, 2, 3):
            hops[p, 0, d].wait_recv()
        count = 1
        for x in after:
            count *= LABELS[x]

        @pl.loop(0, count, unroll=4)
        def _(k):
            fixed = loop_labels(after, k)
            sa[p][index(after, fixed)] = first_sum(p, fixed).astype(bf16)

        for d in (2, 1, 3):
            a2 = REDUCE[p][2][1]
            fixed = labels_of(a2, (at[a2] + d) % 4)
            hop(p, 1, d, sa[p].at[index(after, fixed)], rb[p].at[d - 1])

    def third_hop(p):
        _, last = plan(REDUCE[p])
        _, _, (a1, a2, a3), wave = REDUCE[p]
        for d in (1, 2, 3):
            hops[p, 1, d].wait_recv()
        count = 1
        for x in last:
            count *= LABELS[x]

        @pl.loop(0, count, unroll=True)
        def _(k):
            fixed = loop_labels(last, k)
            total = first_sum(p, {**fixed, **labels_of(a2, at[a2])})
            for d in range(3):
                total += rb[p][(d,) + index(last, fixed)].astype(f32)
            sb[p][index(last, fixed)] = total

        for d in {None: (2, 1, 3), 0: (2,), 1: (1, 3)}[wave]:
            fixed = labels_of(a3, (at[a3] + d) % 4)
            hop(p, 2, d, sb[p].at[index(last, fixed)], rc[p].at[d - 1])

    def finish_sum(parts):
        p = parts[0]
        a3 = REDUCE[p][2][2]
        total = sb[p][index(plan(REDUCE[p])[1], labels_of(a3, at[a3]))]
        for q in parts:
            for d in (1, 2, 3):
                if (q, 2, d) in hops:
                    hops[q, 2, d].wait_recv()
                    total += rc[q][d - 1]
        jsum[:, part_rows(REDUCE[p]), :] = total

    sum_jobs(x_lo, wown)
    first_hop(0)
    first_hop(1)
    wcopy.wait()
    sum_jobs(1 - x_lo, wother)
    for p in (2, 3, 4):
        first_hop(p)
    for c in third.values():
        c.wait_recv()
    total = jnp.zeros((TILE, 2 * TILE), f32)
    row_of = lambda entry: (entry >> 8) & (RB - 1)
    total = running(1, to_workers, row_of, total, 0, SLOTS // 2, (0, 1))
    second_hop(0)
    second_hop(1)
    running(1, to_workers, row_of, total, SLOTS // 2, SLOTS, (0, 1))

    @pl.loop(0, RB)
    def _(j):
        last = slots[4, j] & (SLOTS - 1)
        some = slots[5, j] > 0
        for ref, half in ((away, 1 - x_lo), (kept, x_lo)):
            value = cbuf[last, half]
            ref[j] = jnp.where(some, value, jnp.zeros_like(value))

    acopy = remote(away, rw, osend, orecv, 2, x_mate)
    kcopy = pltpu.make_async_copy(kept, home, in_sem.at[0])
    kcopy.start()
    third_hop(0)
    third_hop(1)
    for p in (2, 3, 4):
        second_hop(p)
    for p in (2, 3, 4):
        third_hop(p)
    finish_sum((0, 2))
    finish_sum((1, 3))
    finish_sum((4,))
    kcopy.wait()
    acopy.wait()
    for copies in (first, second, third, hops):
        for c in copies.values():
            c.wait_send()
    for c in tcopies:
        c.wait_send()


def layer(wemb, wcot, jemb, jcot, wdeg, jdeg, brows, bcols, live, tiles):
    hbm = pl.BlockSpec(memory_space=pl.ANY)
    vmem = pl.BlockSpec(memory_space=pltpu.VMEM)
    ra, sa, rb, sb, rc = [], [], [], [], []
    for part in REDUCE:
        rows = (2, part[1], TILE)
        after, last = (tuple(LABELS[x] for x in labels) + rows for labels in plan(part))
        ra.append(pltpu.VMEM((3,) + after, jnp.bfloat16))
        sa.append(pltpu.VMEM(after, jnp.bfloat16))
        rb.append(pltpu.VMEM((3,) + last, jnp.bfloat16))
        sb.append(pltpu.VMEM(last, jnp.float32))
        rc.append(pltpu.VMEM((3,) + rows, jnp.float32))
    chunks = dims_of("xyz") + (2, TILE, TILE)
    dma = pltpu.SemaphoreType.DMA
    return pl.pallas_call(
        layer_kernel,
        in_specs=[hbm] * 4 + [vmem] * 5 + [hbm],
        out_specs=[hbm, hbm, vmem],
        out_shape=[
            jax.ShapeDtypeStruct((RB, TILE, TILE), jnp.bfloat16),
            jax.ShapeDtypeStruct((RB, TILE, TILE), jnp.bfloat16),
            jax.ShapeDtypeStruct((2, TILE, TILE), jnp.float32),
        ],
        scratch_shapes=[
            pltpu.VMEM((RB, TILE, TILE), jnp.bfloat16),
            pltpu.VMEM((RB, TILE, TILE), jnp.bfloat16),
            pltpu.VMEM((TILE, NW_LOC), jnp.float32),
            pltpu.VMEM((NBUF, TCHUNK, TILE, TILE), jnp.int32),
            pltpu.VMEM((SLOTS, TILE, TILE), jnp.bfloat16),
            pltpu.VMEM(chunks, jnp.bfloat16),
            pltpu.VMEM((TILE, JLOC), jnp.float32),
            pltpu.VMEM((2, 8, NB), jnp.int32),
            pltpu.VMEM((8, SLOTS), jnp.int32),
            pltpu.SMEM((8, SLOTS), jnp.int32),
            pltpu.VMEM((SLOTS, 2, TILE, TILE), jnp.bfloat16),
            pltpu.VMEM(chunks, jnp.bfloat16),
            pltpu.VMEM((RB, TILE, TILE), jnp.bfloat16),
            pltpu.VMEM((RB, TILE, TILE), jnp.bfloat16),
        ]
        + ra
        + sa
        + rb
        + sb
        + rc
        + [
            dma((4,)),
            dma((NBUF,)),
            dma((NCHUNK,)),
            dma((NCHUNK,)),
            dma((3,)),
            dma((3,)),
            dma((66,)),
            dma((66,)),
            dma((45,)),
            dma((45,)),
        ],
        compiler_params=pltpu.CompilerParams(
            collective_id=0, has_side_effects=True, vmem_limit_bytes=60 * 2**20
        ),
        name="layer",
    )(wemb, wcot, jemb, jcot, wdeg, jdeg, brows, bcols, live, tiles)


def finish_kernel(home, rw, jsum, wdeg, jdeg, wout, wgrad, jout, jgrad):
    def write(i, total, scale, out, grad):
        here = slice(i * TILE, (i + 1) * TILE)
        value = jnp.transpose(total) * scale[:, here]
        out[:, here] = value[:64]
        grad[:, here] = value[64:]

    scale = lax.rsqrt(wdeg[...].astype(jnp.float32))
    for i in range(RB):
        write(i, home[i].astype(jnp.float32) + rw[i].astype(jnp.float32), scale, wout, wgrad)
    scale = lax.rsqrt(jdeg[...].astype(jnp.float32))
    for i in range(2):
        write(i, jsum[i], scale, jout, jgrad)


def finish(home, rw, jsum, wdeg, jdeg):
    vmem = pl.BlockSpec(memory_space=pltpu.VMEM)
    return pl.pallas_call(
        finish_kernel,
        in_specs=[vmem] * 5,
        out_specs=[vmem] * 4,
        out_shape=[
            jax.ShapeDtypeStruct((64, NW_LOC), jnp.float32),
            jax.ShapeDtypeStruct((64, NW_LOC), jnp.float32),
            jax.ShapeDtypeStruct((64, JLOC), jnp.float32),
            jax.ShapeDtypeStruct((64, JLOC), jnp.float32),
        ],
        name="finish",
    )(home, rw, jsum, wdeg, jdeg)


def on_device(
    worker_emb,
    job_emb,
    worker_cot,
    job_cot,
    worker_deg,
    job_deg,
    block_rows,
    block_cols,
    block_tiles,
    live_count,
):
    wdeg, jdeg = worker_deg[None, :], job_deg[None, :]
    home, rw, jsum = layer(
        worker_emb.T,
        worker_cot.T,
        job_emb.T,
        job_cot.T,
        wdeg,
        jdeg,
        block_rows[None, :],
        block_cols[None, :],
        live_count,
        block_tiles,
    )
    worker_out, worker_grad, job_out, job_grad = finish(home, rw, jsum, wdeg, jdeg)
    return (worker_out.T, job_out.T, worker_grad.T, job_grad.T)


def solution(mesh):
    return jax.shard_map(
        on_device,
        mesh=mesh,
        in_specs=(
            P("blk", "col"),
            P("blk", "col"),
            P("blk", "col"),
            P("blk", "col"),
            P("blk"),
            P("blk"),
            P(("blk", "col")),
            P(("blk", "col")),
            P(("blk", "col"), None, None),
            P("blk", "col"),
        ),
        out_specs=(P("blk", "col"), P("blk", "col"), P("blk", "col"), P("blk", "col")),
        check_vma=False,
    )
```

```python
import jax
import jax.numpy as jnp
from jax import lax
from jax.experimental import pallas as pl
from jax.experimental.pallas import tpu as pltpu
from jax.sharding import PartitionSpec as P

MESH = pl.DeviceIdType.MESH
TILE = 128
NB = 128
RB = 16
NJB = 64
NW_LOC = RB * TILE
NJ = NJB * TILE
JLOC = 256
SPREAD = ((0, 48, "xyz"), (48, 48, "xzy"), (96, 32, "yzx"))
REDUCE = (
    (0, 48, "yzx", 0),
    (48, 48, "zyx", 0),
    (0, 48, "yzx", 1),
    (48, 48, "zyx", 1),
    (96, 32, "xyz", None),
)
LABELS = {"x_lo": 2, "z": 4, "x_hi": 2, "y": 4}
DIMS = (("x", 2), ("z", 4), ("x", 2), ("y", 4))
TCHUNK = 8
NCHUNK = NB // TCHUNK
NBUF = 4
GROUP = 32
SLOTS = 2 * NB


def position():
    blk = lax.axis_index("blk")
    col = lax.axis_index("col")
    return {
        "z": blk // 8,
        "x": ((blk // 4) % 2) * 2 + col // 2,
        "y": blk % 4,
        "core": col % 2,
    }


def device(at):
    x = at["x"]
    return (at["z"] * 8 + (x // 2) * 4 + at["y"], (x % 2) * 2 + at["core"])


def shifted(at, axis, by):
    return {**at, axis: (at[axis] + by + 4) % 4}


def neighbours(at):
    out = [device(shifted(at, axis, d)) for axis in "xyz" for d in (1, 2, 3)]
    out.append(device({**at, "core": 1 - at["core"]}))
    return out


def dims_of(axes):
    return tuple(n for name, n in DIMS if name in axes)


def pick(axes, fixed):
    index = []
    seen_x = False
    for name, _ in DIMS:
        if name not in axes:
            continue
        if name not in fixed:
            index.append(slice(None))
        elif name == "x":
            index.append(fixed["x"] // 2 if seen_x else fixed["x"] % 2)
        else:
            index.append(fixed[name])
        if name == "x":
            seen_x = True
    return tuple(index)


def part_rows(part):
    return pl.ds(part[0], part[1])


def chunk_part(ref, part, fixed):
    return ref.at[pick("xyz", fixed) + (slice(None), part_rows(part), slice(None))]


def labels_of(axis, coordinate):
    return {"x_lo": coordinate % 2, "x_hi": coordinate // 2} if axis == "x" else {axis: coordinate}


def plan(part):
    _, _, (a1, a2, _), wave = part
    after = [x for x in LABELS if x not in labels_of(a1, 0) and (wave is None or x != "x_lo")]
    return after, [x for x in after if x not in labels_of(a2, 0)]


def index(labels, fixed):
    return tuple(fixed.get(x, slice(None)) for x in labels)


def loop_labels(labels, k):
    fixed = {}
    for x in reversed(labels):
        fixed[x] = k % LABELS[x]
        k = k // LABELS[x]
    return fixed


def block_index(j):
    return (j >> 4, (j >> 3) & 1, (j >> 1) & 3, j & 1)


def order_slots(meta, table):
    lane = lax.broadcasted_iota(jnp.int32, (1, NB), 1)
    place = lax.broadcasted_iota(jnp.int32, (NB, SLOTS), 1)
    block = lax.broadcasted_iota(jnp.int32, (NB, NB), 1)

    def column(row):
        return jnp.transpose(jnp.broadcast_to(row, (NB, NB)))

    def count_down(flags):
        return jnp.sum(jnp.where(flags, 1, 0), axis=0, keepdims=True)

    payloads, cols, rows = [], [], []
    for h in range(2):
        ok = lane < meta[h, 2:3, :]
        r, c = meta[h, 0:1, :], meta[h, 1:2, :]
        payloads.append(lane + h * NB + r * SLOTS + c * (SLOTS * RB))
        cols.append(jnp.where(ok, c, NJB))
        rows.append(jnp.where(ok, r, RB))
    for line, (keys, at) in enumerate(((cols, 2), (rows, 4))):
        unique = [keys[h] * SLOTS + lane + h * NB for h in range(2)]
        across = jnp.broadcast_to(jnp.concatenate(unique, axis=1), (NB, SLOTS))
        rank = jnp.zeros((1, SLOTS), jnp.int32)
        for h in range(2):
            down = column(unique[h])
            rank += count_down(jnp.concatenate([down, down], axis=1) < across)
        ordered = jnp.zeros((1, SLOTS), jnp.int32)
        upto = jnp.zeros((1, NB), jnp.int32)
        count = jnp.zeros((1, NB), jnp.int32)
        for h in range(2):
            spot = column(rank[:, h * NB : (h + 1) * NB])
            hit = place == jnp.concatenate([spot, spot], axis=1)
            value = column(payloads[h])
            value = jnp.concatenate([value, value], axis=1)
            ordered += jnp.sum(jnp.where(hit, value, 0), axis=0, keepdims=True)
            key = column(keys[h])
            upto += count_down(key <= block)
            count += count_down(key == block)
        table[line : line + 1, :] = ordered
        table[at : at + 1, :NB] = jnp.maximum(upto - 1, 0)
        table[at + 1 : at + 2, :NB] = count


def layer_kernel(
    wemb,
    wcot,
    jemb,
    jcot,
    wdeg,
    jdeg,
    brows,
    bcols,
    live,
    tiles,
    home,
    rw,
    jsum,
    wown,
    wother,
    dense_in,
    tin,
    xbuf,
    table,
    rows_in,
    meta,
    order,
    slots,
    cbuf,
    jobs,
    away,
    kept,
    *rest,
):
    ra, sa, rb, sb, rc = (rest[i : i + len(REDUCE)] for i in range(0, 5 * len(REDUCE), len(REDUCE)))
    in_sem, tin_sem, tsend, trecv, osend, orecv, gsend, grecv, ssend, srecv = rest[5 * len(REDUCE) :]
    at = position()
    x_lo = at["x"] % 2
    core = at["core"]
    core_mate = {**at, "core": 1 - core}
    x_mate = {**at, "x": at["x"] + 1 - 2 * x_lo}
    f32, bf16 = jnp.float32, jnp.bfloat16

    def load(i):
        return pltpu.make_async_copy(
            tiles.at[pl.ds(i * TCHUNK, TCHUNK)], tin.at[i % NBUF], tin_sem.at[i % NBUF]
        )

    def remote(src, dst, sems, rems, i, target):
        c = pltpu.make_async_remote_copy(
            src_ref=src,
            dst_ref=dst,
            send_sem=sems.at[i],
            recv_sem=rems.at[i],
            device_id=device(target),
            device_id_type=MESH,
        )
        c.start()
        return c

    barrier = pltpu.get_barrier_semaphore()
    others = neighbours(at)
    for other in others:
        pl.semaphore_signal(barrier, inc=1, device_id=other, device_id_type=MESH)
    ins = [
        pltpu.make_async_copy(jemb, rows_in.at[pl.ds(0, 64)], in_sem.at[0]),
        pltpu.make_async_copy(jcot, rows_in.at[pl.ds(64, 64)], in_sem.at[1]),
        pltpu.make_async_copy(wemb, dense_in.at[pl.ds(0, 64)], in_sem.at[2]),
        pltpu.make_async_copy(wcot, dense_in.at[pl.ds(64, 64)], in_sem.at[3]),
    ]
    for c in ins:
        c.start()
    for i in range(NBUF):
        load(i).start()

    job_scale = lax.rsqrt(jdeg[...].astype(f32))
    worker_scale = lax.rsqrt(wdeg[...].astype(f32))
    meta[core] = jnp.zeros((8, NB), jnp.int32)
    order[...] = jnp.zeros((8, SLOTS), jnp.int32)
    meta[core, 0:1, :] = brows[...]
    meta[core, 1:2, :] = bcols[...]
    meta[core, 2:3, :] = jnp.broadcast_to(live[...], (1, NB))
    ins[0].wait()
    ins[1].wait()
    for i in range(2):
        here = slice(i * TILE, (i + 1) * TILE)
        table[pick("xyz", at) + (i,)] = jnp.transpose(
            rows_in[:, here] * job_scale[:, here]
        ).astype(bf16)
    ins[2].wait()
    ins[3].wait()
    for i in range(RB):
        here = slice(i * TILE, (i + 1) * TILE)
        wown[i] = jnp.transpose(dense_in[:, here] * worker_scale[:, here]).astype(bf16)
    pl.semaphore_wait(barrier, len(others))
    first, second, third = {}, {}, {}
    for d in (1, 3, 2):
        for p in range(3):
            own = chunk_part(table, SPREAD[p], at)
            first[p, d] = remote(
                own, own, gsend, grecv, p * 22 + d - 1, shifted(at, SPREAD[p][2][0], d)
            )
    mcopy = remote(meta.at[core], meta.at[core], osend, orecv, 0, core_mate)
    wcopy = remote(wown, wother, osend, orecv, 1, x_mate)

    tcopies = []

    def chunk(i):
        load(i).wait()
        here = pl.ds(core * NB + i * TCHUNK, TCHUNK)
        xbuf[here] = tin[i % NBUF].astype(f32).astype(bf16)
        if i + NBUF < NCHUNK:
            load(i + NBUF).start()
        tcopies.append(remote(xbuf.at[here], xbuf.at[here], tsend, trecv, i, core_mate))

    def spread(p, g):
        a1, a2, a3 = SPREAD[p][2]
        got = chunk_part(table, SPREAD[p], {a2: (at[a2] - g + 4) % 4, a3: at[a3]})
        for d in (1, 3, 2):
            third[p, g, d] = remote(
                got, got, gsend, grecv, p * 22 + 6 + g * 4 + d - 1, shifted(at, a3, d)
            )

    for p in range(3):
        a1, a2, a3 = SPREAD[p][2]
        for d in (1, 2, 3):
            first[p, d].wait_recv()
        own = chunk_part(table, SPREAD[p], {a2: at[a2], a3: at[a3]})
        for d in (1, 3, 2):
            second[p, d] = remote(own, own, gsend, grecv, p * 22 + 3 + d - 1, shifted(at, a2, d))
    for p in range(3):
        spread(p, 0)
    for i in range(NCHUNK // 2):
        chunk(i)
    for g in (1, 3, 2):
        for p in range(3):
            second[p, g].wait_recv()
            spread(p, g)
    for i in range(NCHUNK // 2, NCHUNK):
        chunk(i)
    mcopy.wait()
    order_slots(meta, order)
    to_scalars = pltpu.make_async_copy(order, slots, in_sem.at[0])
    to_scalars.start()
    to_scalars.wait()
    for c in tcopies:
        c.wait_recv()

    def running(line, product, key, total, start, stop, halves):
        def step(q, total):
            for g in range(GROUP):
                k = q * GROUP + g
                entry = slots[line, k]
                before = slots[line, jnp.maximum(k - 1, 0)]
                fresh = key(entry) != key(before)
                total = jnp.where(fresh, 0.0, total) + product(
                    entry & (SLOTS - 1), (entry >> 8) & (RB - 1), (entry >> 12) & (NJB - 1)
                )
                for i, half in enumerate(halves):
                    cbuf[k, half] = total[:, i * TILE : (i + 1) * TILE].astype(bf16)
            return total

        return lax.fori_loop(start // GROUP, stop // GROUP, step, total)

    def to_workers(s, r, c):
        i = block_index(c)
        rows = jnp.concatenate([table[(0,) + i], table[(1,) + i]], axis=1)
        return jnp.dot(xbuf[s], rows, preferred_element_type=f32)

    def sum_jobs(half, workers):
        def to_jobs(s, r, c):
            return lax.dot_general(
                xbuf[s], workers[r], (((0,), (0,)), ((), ())), preferred_element_type=f32
            )

        total = jnp.zeros((TILE, TILE), f32)
        running(0, to_jobs, lambda entry: entry >> 12, total, 0, SLOTS, (0,))

        @pl.loop(0, NJB, unroll=4)
        def _(j):
            last = slots[2, j] & (SLOTS - 1)
            some = slots[3, j] > 0
            value = cbuf[last, 0]
            jobs[(half,) + block_index(j)] = jnp.where(some, value, jnp.zeros_like(value))

    hops = {}
    wave_lo = (x_lo, 1 - x_lo)

    def hop(p, stage, d, src, dst):
        target = shifted(at, REDUCE[p][2][stage], d)
        hops[p, stage, d] = remote(src, dst, ssend, srecv, p * 9 + stage * 3 + d - 1, target)

    def fixed_of(p, axis, by):
        fixed = labels_of(axis, (at[axis] + by) % 4)
        if REDUCE[p][3] is not None and axis != "x":
            fixed["x_lo"] = wave_lo[REDUCE[p][3]]
        return fixed

    def first_hop(p):
        rows = (slice(None), part_rows(REDUCE[p]), slice(None))
        for d in (2, 1, 3):
            fixed = fixed_of(p, REDUCE[p][2][0], d)
            hop(p, 0, d, jobs.at[index(LABELS, fixed) + rows], ra[p].at[d - 1])

    def first_sum(p, fixed):
        own = {**fixed_of(p, REDUCE[p][2][0], 0), **fixed}
        rows = (slice(None), part_rows(REDUCE[p]), slice(None))
        total = jobs[index(LABELS, own) + rows].astype(f32)
        for d in range(3):
            total += ra[p][(d,) + index(plan(REDUCE[p])[0], fixed)].astype(f32)
        return total

    def second_hop(p):
        after, _ = plan(REDUCE[p])
        for d in (1, 2, 3):
            hops[p, 0, d].wait_recv()
        count = 1
        for x in after:
            count *= LABELS[x]

        @pl.loop(0, count, unroll=4)
        def _(k):
            fixed = loop_labels(after, k)
            sa[p][index(after, fixed)] = first_sum(p, fixed).astype(bf16)

        for d in (2, 1, 3):
            a2 = REDUCE[p][2][1]
            fixed = labels_of(a2, (at[a2] + d) % 4)
            hop(p, 1, d, sa[p].at[index(after, fixed)], rb[p].at[d - 1])

    def third_hop(p):
        _, last = plan(REDUCE[p])
        _, _, (a1, a2, a3), wave = REDUCE[p]
        for d in (1, 2, 3):
            hops[p, 1, d].wait_recv()
        count = 1
        for x in last:
            count *= LABELS[x]

        @pl.loop(0, count, unroll=True)
        def _(k):
            fixed = loop_labels(last, k)
            total = first_sum(p, {**fixed, **labels_of(a2, at[a2])})
            for d in range(3):
                total += rb[p][(d,) + index(last, fixed)].astype(f32)
            sb[p][index(last, fixed)] = total

        for d in {None: (2, 1, 3), 0: (2,), 1: (1, 3)}[wave]:
            fixed = labels_of(a3, (at[a3] + d) % 4)
            hop(p, 2, d, sb[p].at[index(last, fixed)], rc[p].at[d - 1])

    def finish_sum(parts):
        p = parts[0]
        a3 = REDUCE[p][2][2]
        total = sb[p][index(plan(REDUCE[p])[1], labels_of(a3, at[a3]))]
        for q in parts:
            for d in (1, 2, 3):
                if (q, 2, d) in hops:
                    hops[q, 2, d].wait_recv()
                    total += rc[q][d - 1]
        jsum[:, part_rows(REDUCE[p]), :] = total

    sum_jobs(x_lo, wown)
    first_hop(0)
    first_hop(1)
    wcopy.wait()
    sum_jobs(1 - x_lo, wother)
    for p in (4, 2, 3):
        first_hop(p)
    for c in third.values():
        c.wait_recv()
    total = jnp.zeros((TILE, 2 * TILE), f32)
    row_of = lambda entry: (entry >> 8) & (RB - 1)
    total = running(1, to_workers, row_of, total, 0, SLOTS // 2, (0, 1))
    second_hop(0)
    second_hop(1)
    running(1, to_workers, row_of, total, SLOTS // 2, SLOTS, (0, 1))

    @pl.loop(0, RB)
    def _(j):
        last = slots[4, j] & (SLOTS - 1)
        some = slots[5, j] > 0
        for ref, half in ((away, 1 - x_lo), (kept, x_lo)):
            value = cbuf[last, half]
            ref[j] = jnp.where(some, value, jnp.zeros_like(value))

    acopy = remote(away, rw, osend, orecv, 2, x_mate)
    kcopy = pltpu.make_async_copy(kept, home, in_sem.at[0])
    kcopy.start()
    for p in (4, 2, 3):
        second_hop(p)
    for p in (0, 1, 4, 2, 3):
        third_hop(p)
    finish_sum((0, 2))
    finish_sum((1, 3))
    finish_sum((4,))
    kcopy.wait()
    acopy.wait()
    for copies in (first, second, third, hops):
        for c in copies.values():
            c.wait_send()
    for c in tcopies:
        c.wait_send()


def layer(wemb, wcot, jemb, jcot, wdeg, jdeg, brows, bcols, live, tiles):
    hbm = pl.BlockSpec(memory_space=pl.ANY)
    vmem = pl.BlockSpec(memory_space=pltpu.VMEM)
    ra, sa, rb, sb, rc = [], [], [], [], []
    for part in REDUCE:
        rows = (2, part[1], TILE)
        after, last = (tuple(LABELS[x] for x in labels) + rows for labels in plan(part))
        ra.append(pltpu.VMEM((3,) + after, jnp.bfloat16))
        sa.append(pltpu.VMEM(after, jnp.bfloat16))
        rb.append(pltpu.VMEM((3,) + last, jnp.bfloat16))
        sb.append(pltpu.VMEM(last, jnp.float32))
        rc.append(pltpu.VMEM((3,) + rows, jnp.float32))
    chunks = dims_of("xyz") + (2, TILE, TILE)
    dma = pltpu.SemaphoreType.DMA
    return pl.pallas_call(
        layer_kernel,
        in_specs=[hbm] * 4 + [vmem] * 5 + [hbm],
        out_specs=[hbm, hbm, vmem],
        out_shape=[
            jax.ShapeDtypeStruct((RB, TILE, TILE), jnp.bfloat16),
            jax.ShapeDtypeStruct((RB, TILE, TILE), jnp.bfloat16),
            jax.ShapeDtypeStruct((2, TILE, TILE), jnp.float32),
        ],
        scratch_shapes=[
            pltpu.VMEM((RB, TILE, TILE), jnp.bfloat16),
            pltpu.VMEM((RB, TILE, TILE), jnp.bfloat16),
            pltpu.VMEM((TILE, NW_LOC), jnp.float32),
            pltpu.VMEM((NBUF, TCHUNK, TILE, TILE), jnp.int32),
            pltpu.VMEM((SLOTS, TILE, TILE), jnp.bfloat16),
            pltpu.VMEM(chunks, jnp.bfloat16),
            pltpu.VMEM((TILE, JLOC), jnp.float32),
            pltpu.VMEM((2, 8, NB), jnp.int32),
            pltpu.VMEM((8, SLOTS), jnp.int32),
            pltpu.SMEM((8, SLOTS), jnp.int32),
            pltpu.VMEM((SLOTS, 2, TILE, TILE), jnp.bfloat16),
            pltpu.VMEM(chunks, jnp.bfloat16),
            pltpu.VMEM((RB, TILE, TILE), jnp.bfloat16),
            pltpu.VMEM((RB, TILE, TILE), jnp.bfloat16),
        ]
        + ra
        + sa
        + rb
        + sb
        + rc
        + [
            dma((4,)),
            dma((NBUF,)),
            dma((NCHUNK,)),
            dma((NCHUNK,)),
            dma((3,)),
            dma((3,)),
            dma((66,)),
            dma((66,)),
            dma((45,)),
            dma((45,)),
        ],
        compiler_params=pltpu.CompilerParams(
            collective_id=0, has_side_effects=True, vmem_limit_bytes=60 * 2**20
        ),
        name="layer",
    )(wemb, wcot, jemb, jcot, wdeg, jdeg, brows, bcols, live, tiles)


def finish_kernel(home, rw, jsum, wdeg, jdeg, wout, wgrad, jout, jgrad):
    def write(i, total, scale, out, grad):
        here = slice(i * TILE, (i + 1) * TILE)
        value = jnp.transpose(total) * scale[:, here]
        out[:, here] = value[:64]
        grad[:, here] = value[64:]

    scale = lax.rsqrt(wdeg[...].astype(jnp.float32))
    for i in range(RB):
        write(i, home[i].astype(jnp.float32) + rw[i].astype(jnp.float32), scale, wout, wgrad)
    scale = lax.rsqrt(jdeg[...].astype(jnp.float32))
    for i in range(2):
        write(i, jsum[i], scale, jout, jgrad)


def finish(home, rw, jsum, wdeg, jdeg):
    vmem = pl.BlockSpec(memory_space=pltpu.VMEM)
    return pl.pallas_call(
        finish_kernel,
        in_specs=[vmem] * 5,
        out_specs=[vmem] * 4,
        out_shape=[
            jax.ShapeDtypeStruct((64, NW_LOC), jnp.float32),
            jax.ShapeDtypeStruct((64, NW_LOC), jnp.float32),
            jax.ShapeDtypeStruct((64, JLOC), jnp.float32),
            jax.ShapeDtypeStruct((64, JLOC), jnp.float32),
        ],
        name="finish",
    )(home, rw, jsum, wdeg, jdeg)


def on_device(
    worker_emb,
    job_emb,
    worker_cot,
    job_cot,
    worker_deg,
    job_deg,
    block_rows,
    block_cols,
    block_tiles,
    live_count,
):
    wdeg, jdeg = worker_deg[None, :], job_deg[None, :]
    home, rw, jsum = layer(
        worker_emb.T,
        worker_cot.T,
        job_emb.T,
        job_cot.T,
        wdeg,
        jdeg,
        block_rows[None, :],
        block_cols[None, :],
        live_count,
        block_tiles,
    )
    worker_out, worker_grad, job_out, job_grad = finish(home, rw, jsum, wdeg, jdeg)
    return (worker_out.T, job_out.T, worker_grad.T, job_grad.T)


def solution(mesh):
    return jax.shard_map(
        on_device,
        mesh=mesh,
        in_specs=(
            P("blk", "col"),
            P("blk", "col"),
            P("blk", "col"),
            P("blk", "col"),
            P("blk"),
            P("blk"),
            P(("blk", "col")),
            P(("blk", "col")),
            P(("blk", "col"), None, None),
            P("blk", "col"),
        ),
        out_specs=(P("blk", "col"), P("blk", "col"), P("blk", "col"), P("blk", "col")),
        check_vma=False,
    )
```

```python
import jax
import jax.numpy as jnp
from jax import lax
from jax.experimental import pallas as pl
from jax.experimental.pallas import tpu as pltpu
from jax.sharding import PartitionSpec as P

MESH = pl.DeviceIdType.MESH
TILE = 128
NB = 128
RB = 16
NJB = 64
NW_LOC = RB * TILE
NJ = NJB * TILE
JLOC = 256
SPREAD = ((0, 48, "xyz"), (48, 48, "xzy"), (96, 32, "yzx"))
REDUCE = (
    (0, 48, "yzx", 0),
    (48, 48, "zyx", 0),
    (0, 48, "yzx", 1),
    (48, 48, "zyx", 1),
    (96, 32, "xyz", None),
)
LABELS = {"x_lo": 2, "z": 4, "x_hi": 2, "y": 4}
DIMS = (("x", 2), ("z", 4), ("x", 2), ("y", 4))
TCHUNK = 8
NCHUNK = NB // TCHUNK
NBUF = 4
GROUP = 32
SLOTS = 2 * NB


def position():
    blk = lax.axis_index("blk")
    col = lax.axis_index("col")
    return {
        "z": blk // 8,
        "x": ((blk // 4) % 2) * 2 + col // 2,
        "y": blk % 4,
        "core": col % 2,
    }


def device(at):
    x = at["x"]
    return (at["z"] * 8 + (x // 2) * 4 + at["y"], (x % 2) * 2 + at["core"])


def shifted(at, axis, by):
    return {**at, axis: (at[axis] + by + 4) % 4}


def neighbours(at):
    out = [device(shifted(at, axis, d)) for axis in "xyz" for d in (1, 2, 3)]
    out.append(device({**at, "core": 1 - at["core"]}))
    return out


def dims_of(axes):
    return tuple(n for name, n in DIMS if name in axes)


def pick(axes, fixed):
    index = []
    seen_x = False
    for name, _ in DIMS:
        if name not in axes:
            continue
        if name not in fixed:
            index.append(slice(None))
        elif name == "x":
            index.append(fixed["x"] // 2 if seen_x else fixed["x"] % 2)
        else:
            index.append(fixed[name])
        if name == "x":
            seen_x = True
    return tuple(index)


def part_rows(part):
    return pl.ds(part[0], part[1])


def chunk_part(ref, part, fixed):
    return ref.at[pick("xyz", fixed) + (slice(None), part_rows(part), slice(None))]


def labels_of(axis, coordinate):
    return {"x_lo": coordinate % 2, "x_hi": coordinate // 2} if axis == "x" else {axis: coordinate}


def plan(part):
    _, _, (a1, a2, _), wave = part
    after = [x for x in LABELS if x not in labels_of(a1, 0) and (wave is None or x != "x_lo")]
    return after, [x for x in after if x not in labels_of(a2, 0)]


def index(labels, fixed):
    return tuple(fixed.get(x, slice(None)) for x in labels)


def loop_labels(labels, k):
    fixed = {}
    for x in reversed(labels):
        fixed[x] = k % LABELS[x]
        k = k // LABELS[x]
    return fixed


def chunks_of(labels):
    count = 1
    for x in labels:
        count *= LABELS[x]
    return count


def block_index(j):
    return (j >> 4, (j >> 3) & 1, (j >> 1) & 3, j & 1)


def order_slots(meta, table):
    lane = lax.broadcasted_iota(jnp.int32, (1, NB), 1)
    place = lax.broadcasted_iota(jnp.int32, (NB, SLOTS), 1)
    block = lax.broadcasted_iota(jnp.int32, (NB, NB), 1)

    def column(row):
        return jnp.transpose(jnp.broadcast_to(row, (NB, NB)))

    def count_down(flags):
        return jnp.sum(jnp.where(flags, 1, 0), axis=0, keepdims=True)

    payloads, cols, rows = [], [], []
    for h in range(2):
        ok = lane < meta[h, 2:3, :]
        r, c = meta[h, 0:1, :], meta[h, 1:2, :]
        payloads.append(lane + h * NB + r * SLOTS + c * (SLOTS * RB))
        cols.append(jnp.where(ok, c, NJB))
        rows.append(jnp.where(ok, r, RB))
    for line, (keys, at) in enumerate(((cols, 2), (rows, 4))):
        unique = [keys[h] * SLOTS + lane + h * NB for h in range(2)]
        across = jnp.broadcast_to(jnp.concatenate(unique, axis=1), (NB, SLOTS))
        rank = jnp.zeros((1, SLOTS), jnp.int32)
        for h in range(2):
            down = column(unique[h])
            rank += count_down(jnp.concatenate([down, down], axis=1) < across)
        ordered = jnp.zeros((1, SLOTS), jnp.int32)
        upto = jnp.zeros((1, NB), jnp.int32)
        count = jnp.zeros((1, NB), jnp.int32)
        for h in range(2):
            spot = column(rank[:, h * NB : (h + 1) * NB])
            hit = place == jnp.concatenate([spot, spot], axis=1)
            value = column(payloads[h])
            value = jnp.concatenate([value, value], axis=1)
            ordered += jnp.sum(jnp.where(hit, value, 0), axis=0, keepdims=True)
            key = column(keys[h])
            upto += count_down(key <= block)
            count += count_down(key == block)
        table[line : line + 1, :] = ordered
        table[at : at + 1, :NB] = jnp.maximum(upto - 1, 0)
        table[at + 1 : at + 2, :NB] = count


def layer_kernel(
    wemb,
    wcot,
    jemb,
    jcot,
    wdeg,
    jdeg,
    brows,
    bcols,
    live,
    tiles,
    home,
    rw,
    jsum,
    wown,
    wother,
    dense_in,
    tin,
    xbuf,
    table,
    rows_in,
    meta,
    order,
    slots,
    cbuf,
    jobs,
    away,
    kept,
    *rest,
):
    n = len(REDUCE)
    ra, fs, sa, rb, sb, rc = (rest[i : i + n] for i in range(0, 6 * n, n))
    in_sem, tin_sem, tsend, trecv, osend, orecv, gsend, grecv, ssend, srecv = rest[6 * n :]
    at = position()
    x_lo = at["x"] % 2
    core = at["core"]
    core_mate = {**at, "core": 1 - core}
    x_mate = {**at, "x": at["x"] + 1 - 2 * x_lo}
    f32, bf16 = jnp.float32, jnp.bfloat16

    def load(i):
        return pltpu.make_async_copy(
            tiles.at[pl.ds(i * TCHUNK, TCHUNK)], tin.at[i % NBUF], tin_sem.at[i % NBUF]
        )

    def remote(src, dst, sems, rems, i, target):
        c = pltpu.make_async_remote_copy(
            src_ref=src,
            dst_ref=dst,
            send_sem=sems.at[i],
            recv_sem=rems.at[i],
            device_id=device(target),
            device_id_type=MESH,
        )
        c.start()
        return c

    barrier = pltpu.get_barrier_semaphore()
    others = neighbours(at)
    for other in others:
        pl.semaphore_signal(barrier, inc=1, device_id=other, device_id_type=MESH)
    ins = [
        pltpu.make_async_copy(jemb, rows_in.at[pl.ds(0, 64)], in_sem.at[0]),
        pltpu.make_async_copy(jcot, rows_in.at[pl.ds(64, 64)], in_sem.at[1]),
        pltpu.make_async_copy(wemb, dense_in.at[pl.ds(0, 64)], in_sem.at[2]),
        pltpu.make_async_copy(wcot, dense_in.at[pl.ds(64, 64)], in_sem.at[3]),
    ]
    for c in ins:
        c.start()
    for i in range(NBUF):
        load(i).start()

    job_scale = lax.rsqrt(jdeg[...].astype(f32))
    worker_scale = lax.rsqrt(wdeg[...].astype(f32))
    meta[core] = jnp.zeros((8, NB), jnp.int32)
    order[...] = jnp.zeros((8, SLOTS), jnp.int32)
    meta[core, 0:1, :] = brows[...]
    meta[core, 1:2, :] = bcols[...]
    meta[core, 2:3, :] = jnp.broadcast_to(live[...], (1, NB))
    ins[0].wait()
    ins[1].wait()
    for i in range(2):
        here = slice(i * TILE, (i + 1) * TILE)
        table[pick("xyz", at) + (i,)] = jnp.transpose(
            rows_in[:, here] * job_scale[:, here]
        ).astype(bf16)
    pl.semaphore_wait(barrier, len(others))
    first, second, third = {}, {}, {}
    for d in (1, 3, 2):
        for p in range(3):
            own = chunk_part(table, SPREAD[p], at)
            first[p, d] = remote(
                own, own, gsend, grecv, p * 22 + d - 1, shifted(at, SPREAD[p][2][0], d)
            )
    mcopy = remote(meta.at[core], meta.at[core], osend, orecv, 0, core_mate)
    ins[2].wait()
    ins[3].wait()
    for i in range(RB):
        here = slice(i * TILE, (i + 1) * TILE)
        wown[i] = jnp.transpose(dense_in[:, here] * worker_scale[:, here]).astype(bf16)
    wcopy = remote(wown, wother, osend, orecv, 1, x_mate)

    tcopies = []

    def chunk(i):
        load(i).wait()
        here = pl.ds(core * NB + i * TCHUNK, TCHUNK)
        xbuf[here] = tin[i % NBUF].astype(f32).astype(bf16)
        if i + NBUF < NCHUNK:
            load(i + NBUF).start()
        tcopies.append(remote(xbuf.at[here], xbuf.at[here], tsend, trecv, i, core_mate))

    def spread(p, g):
        a1, a2, a3 = SPREAD[p][2]
        got = chunk_part(table, SPREAD[p], {a2: (at[a2] - g + 4) % 4, a3: at[a3]})
        for d in (1, 3, 2):
            third[p, g, d] = remote(
                got, got, gsend, grecv, p * 22 + 6 + g * 4 + d - 1, shifted(at, a3, d)
            )

    for p in range(3):
        a1, a2, a3 = SPREAD[p][2]
        for d in (1, 2, 3):
            first[p, d].wait_recv()
        own = chunk_part(table, SPREAD[p], {a2: at[a2], a3: at[a3]})
        for d in (1, 3, 2):
            second[p, d] = remote(own, own, gsend, grecv, p * 22 + 3 + d - 1, shifted(at, a2, d))
    for p in range(3):
        spread(p, 0)
    for i in range(NCHUNK // 2):
        chunk(i)
    for g in (1, 3, 2):
        for p in range(3):
            second[p, g].wait_recv()
            spread(p, g)
    for i in range(NCHUNK // 2, NCHUNK):
        chunk(i)
    mcopy.wait()
    order_slots(meta, order)
    to_scalars = pltpu.make_async_copy(order, slots, in_sem.at[0])
    to_scalars.start()
    to_scalars.wait()
    for c in tcopies:
        c.wait_recv()

    def running(line, product, key, total, start, stop, halves):
        def step(q, total):
            for g in range(GROUP):
                k = q * GROUP + g
                entry = slots[line, k]
                before = slots[line, jnp.maximum(k - 1, 0)]
                fresh = key(entry) != key(before)
                total = jnp.where(fresh, 0.0, total) + product(
                    entry & (SLOTS - 1), (entry >> 8) & (RB - 1), (entry >> 12) & (NJB - 1)
                )
                for i, half in enumerate(halves):
                    cbuf[k, half] = total[:, i * TILE : (i + 1) * TILE].astype(bf16)
            return total

        return lax.fori_loop(start // GROUP, stop // GROUP, step, total)

    def to_workers(s, r, c):
        i = block_index(c)
        rows = jnp.concatenate([table[(0,) + i], table[(1,) + i]], axis=1)
        return jnp.dot(xbuf[s], rows, preferred_element_type=f32)

    def sum_jobs(half, workers):
        def to_jobs(s, r, c):
            return lax.dot_general(
                xbuf[s], workers[r], (((0,), (0,)), ((), ())), preferred_element_type=f32
            )

        total = jnp.zeros((TILE, TILE), f32)
        running(0, to_jobs, lambda entry: entry >> 12, total, 0, SLOTS, (0,))

        @pl.loop(0, NJB, unroll=4)
        def _(j):
            last = slots[2, j] & (SLOTS - 1)
            some = slots[3, j] > 0
            value = cbuf[last, 0]
            jobs[(half,) + block_index(j)] = jnp.where(some, value, jnp.zeros_like(value))

    hops = {}
    wave_lo = (x_lo, 1 - x_lo)

    def hop(p, name, stage, d, sem, src, dst):
        target = shifted(at, REDUCE[p][2][stage], d)
        hops[p, name] = remote(src, dst, ssend, srecv, p * 12 + sem, target)

    def fixed_of(p, axis, by):
        fixed = labels_of(axis, (at[axis] + by) % 4)
        if REDUCE[p][3] is not None and axis != "x":
            fixed["x_lo"] = wave_lo[REDUCE[p][3]]
        return fixed

    def halves_of(p, d):
        fixed = fixed_of(p, REDUCE[p][2][0], d)
        rows = part_rows(REDUCE[p])
        return [jobs.at[index(LABELS, fixed) + (half, rows, slice(None))] for half in (0, 1)]

    def slot_half(ref, p, half):
        return ref.at[index(plan(REDUCE[p])[0], {}) + (half,)]

    def first_hop(p):
        far, right, left = halves_of(p, 2), halves_of(p, 1), halves_of(p, 3)
        hop(p, "far_r", 0, 1, 0, far[0], slot_half(ra[p].at[2], p, 0))
        hop(p, "far_l", 0, 3, 1, far[1], slot_half(ra[p].at[2], p, 1))
        hop(p, "right", 0, 1, 2, right[1], slot_half(ra[p].at[0], p, 1))
        hop(p, "left", 0, 3, 3, left[0], slot_half(ra[p].at[1], p, 0))

    def add_far(p):
        a1 = REDUCE[p][2][0]
        after, _ = plan(REDUCE[p])
        hops[p, "far_r"].wait_recv()
        hops[p, "far_l"].wait_recv()

        @pl.loop(0, chunks_of(after), unroll=4)
        def _(k):
            fixed = loop_labels(after, k)
            for half, d in ((0, 1), (1, 3)):
                theirs = {**fixed_of(p, a1, d), **fixed}
                here = index(LABELS, theirs) + (half, part_rows(REDUCE[p]), slice(None))
                place = index(after, fixed) + (half,)
                total = jobs[here].astype(f32) + ra[p][(2,) + place].astype(f32)
                fs[p][place] = total.astype(bf16)

        hop(p, "sum_r", 0, 1, 4, slot_half(fs[p], p, 0), slot_half(ra[p].at[0], p, 0))
        hop(p, "sum_l", 0, 3, 5, slot_half(fs[p], p, 1), slot_half(ra[p].at[1], p, 1))

    def first_sum(p, fixed):
        own = {**fixed_of(p, REDUCE[p][2][0], 0), **fixed}
        rows = (slice(None), part_rows(REDUCE[p]), slice(None))
        total = jobs[index(LABELS, own) + rows].astype(f32)
        for slot in range(2):
            total += ra[p][(slot,) + index(plan(REDUCE[p])[0], fixed)].astype(f32)
        return total

    def second_hop(p):
        after, _ = plan(REDUCE[p])
        for name in ("right", "left", "sum_r", "sum_l"):
            hops[p, name].wait_recv()

        @pl.loop(0, chunks_of(after), unroll=4)
        def _(k):
            fixed = loop_labels(after, k)
            sa[p][index(after, fixed)] = first_sum(p, fixed).astype(bf16)

        for d in (2, 1, 3):
            a2 = REDUCE[p][2][1]
            fixed = labels_of(a2, (at[a2] + d) % 4)
            hop(p, (1, d), 1, d, 5 + d, sa[p].at[index(after, fixed)], rb[p].at[d - 1])

    def third_hop(p):
        _, last = plan(REDUCE[p])
        _, _, (a1, a2, a3), wave = REDUCE[p]
        for d in (1, 2, 3):
            hops[p, (1, d)].wait_recv()

        @pl.loop(0, chunks_of(last), unroll=True)
        def _(k):
            fixed = loop_labels(last, k)
            total = first_sum(p, {**fixed, **labels_of(a2, at[a2])})
            for d in range(3):
                total += rb[p][(d,) + index(last, fixed)].astype(f32)
            sb[p][index(last, fixed)] = total

        for d in {None: (2, 1, 3), 0: (2,), 1: (1, 3)}[wave]:
            fixed = labels_of(a3, (at[a3] + d) % 4)
            hop(p, (2, d), 2, d, 8 + d, sb[p].at[index(last, fixed)], rc[p].at[d - 1])

    def finish_sum(parts):
        p = parts[0]
        a3 = REDUCE[p][2][2]
        total = sb[p][index(plan(REDUCE[p])[1], labels_of(a3, at[a3]))]
        for q in parts:
            for d in (1, 2, 3):
                if (q, (2, d)) in hops:
                    hops[q, (2, d)].wait_recv()
                    total += rc[q][d - 1]
        jsum[:, part_rows(REDUCE[p]), :] = total

    sum_jobs(x_lo, wown)
    first_hop(0)
    first_hop(1)
    wcopy.wait()
    sum_jobs(1 - x_lo, wother)
    for p in (2, 3, 4):
        first_hop(p)
    add_far(0)
    add_far(1)
    for c in third.values():
        c.wait_recv()
    total = jnp.zeros((TILE, 2 * TILE), f32)
    row_of = lambda entry: (entry >> 8) & (RB - 1)
    total = running(1, to_workers, row_of, total, 0, SLOTS // 2, (0, 1))
    for p in (2, 3, 4):
        add_far(p)
    running(1, to_workers, row_of, total, SLOTS // 2, SLOTS, (0, 1))

    @pl.loop(0, RB)
    def _(j):
        last = slots[4, j] & (SLOTS - 1)
        some = slots[5, j] > 0
        for ref, half in ((away, 1 - x_lo), (kept, x_lo)):
            value = cbuf[last, half]
            ref[j] = jnp.where(some, value, jnp.zeros_like(value))

    acopy = remote(away, rw, osend, orecv, 2, x_mate)
    kcopy = pltpu.make_async_copy(kept, home, in_sem.at[0])
    kcopy.start()
    for p in range(len(REDUCE)):
        second_hop(p)
    for p in range(len(REDUCE)):
        third_hop(p)
    finish_sum((0, 2))
    finish_sum((1, 3))
    finish_sum((4,))
    kcopy.wait()
    acopy.wait()
    for copies in (first, second, third, hops):
        for c in copies.values():
            c.wait_send()
    for c in tcopies:
        c.wait_send()


def layer(wemb, wcot, jemb, jcot, wdeg, jdeg, brows, bcols, live, tiles):
    hbm = pl.BlockSpec(memory_space=pl.ANY)
    vmem = pl.BlockSpec(memory_space=pltpu.VMEM)
    ra, fs, sa, rb, sb, rc = [], [], [], [], [], []
    for part in REDUCE:
        rows = (2, part[1], TILE)
        after, last = (tuple(LABELS[x] for x in labels) + rows for labels in plan(part))
        ra.append(pltpu.VMEM((3,) + after, jnp.bfloat16))
        fs.append(pltpu.VMEM(after, jnp.bfloat16))
        sa.append(pltpu.VMEM(after, jnp.bfloat16))
        rb.append(pltpu.VMEM((3,) + last, jnp.bfloat16))
        sb.append(pltpu.VMEM(last, jnp.float32))
        rc.append(pltpu.VMEM((3,) + rows, jnp.float32))
    chunks = dims_of("xyz") + (2, TILE, TILE)
    dma = pltpu.SemaphoreType.DMA
    return pl.pallas_call(
        layer_kernel,
        in_specs=[hbm] * 4 + [vmem] * 5 + [hbm],
        out_specs=[hbm, hbm, vmem],
        out_shape=[
            jax.ShapeDtypeStruct((RB, TILE, TILE), jnp.bfloat16),
            jax.ShapeDtypeStruct((RB, TILE, TILE), jnp.bfloat16),
            jax.ShapeDtypeStruct((2, TILE, TILE), jnp.float32),
        ],
        scratch_shapes=[
            pltpu.VMEM((RB, TILE, TILE), jnp.bfloat16),
            pltpu.VMEM((RB, TILE, TILE), jnp.bfloat16),
            pltpu.VMEM((TILE, NW_LOC), jnp.float32),
            pltpu.VMEM((NBUF, TCHUNK, TILE, TILE), jnp.int32),
            pltpu.VMEM((SLOTS, TILE, TILE), jnp.bfloat16),
            pltpu.VMEM(chunks, jnp.bfloat16),
            pltpu.VMEM((TILE, JLOC), jnp.float32),
            pltpu.VMEM((2, 8, NB), jnp.int32),
            pltpu.VMEM((8, SLOTS), jnp.int32),
            pltpu.SMEM((8, SLOTS), jnp.int32),
            pltpu.VMEM((SLOTS, 2, TILE, TILE), jnp.bfloat16),
            pltpu.VMEM(chunks, jnp.bfloat16),
            pltpu.VMEM((RB, TILE, TILE), jnp.bfloat16),
            pltpu.VMEM((RB, TILE, TILE), jnp.bfloat16),
        ]
        + ra
        + fs
        + sa
        + rb
        + sb
        + rc
        + [
            dma((4,)),
            dma((NBUF,)),
            dma((NCHUNK,)),
            dma((NCHUNK,)),
            dma((3,)),
            dma((3,)),
            dma((66,)),
            dma((66,)),
            dma((60,)),
            dma((60,)),
        ],
        compiler_params=pltpu.CompilerParams(
            collective_id=0, has_side_effects=True, vmem_limit_bytes=60 * 2**20
        ),
        name="layer",
    )(wemb, wcot, jemb, jcot, wdeg, jdeg, brows, bcols, live, tiles)


def finish_kernel(home, rw, jsum, wdeg, jdeg, wout, wgrad, jout, jgrad):
    def write(i, total, scale, out, grad):
        here = slice(i * TILE, (i + 1) * TILE)
        value = jnp.transpose(total) * scale[:, here]
        out[:, here] = value[:64]
        grad[:, here] = value[64:]

    scale = lax.rsqrt(wdeg[...].astype(jnp.float32))
    for i in range(RB):
        write(i, home[i].astype(jnp.float32) + rw[i].astype(jnp.float32), scale, wout, wgrad)
    scale = lax.rsqrt(jdeg[...].astype(jnp.float32))
    for i in range(2):
        write(i, jsum[i], scale, jout, jgrad)


def finish(home, rw, jsum, wdeg, jdeg):
    vmem = pl.BlockSpec(memory_space=pltpu.VMEM)
    return pl.pallas_call(
        finish_kernel,
        in_specs=[vmem] * 5,
        out_specs=[vmem] * 4,
        out_shape=[
            jax.ShapeDtypeStruct((64, NW_LOC), jnp.float32),
            jax.ShapeDtypeStruct((64, NW_LOC), jnp.float32),
            jax.ShapeDtypeStruct((64, JLOC), jnp.float32),
            jax.ShapeDtypeStruct((64, JLOC), jnp.float32),
        ],
        name="finish",
    )(home, rw, jsum, wdeg, jdeg)


def on_device(
    worker_emb,
    job_emb,
    worker_cot,
    job_cot,
    worker_deg,
    job_deg,
    block_rows,
    block_cols,
    block_tiles,
    live_count,
):
    wdeg, jdeg = worker_deg[None, :], job_deg[None, :]
    home, rw, jsum = layer(
        worker_emb.T,
        worker_cot.T,
        job_emb.T,
        job_cot.T,
        wdeg,
        jdeg,
        block_rows[None, :],
        block_cols[None, :],
        live_count,
        block_tiles,
    )
    worker_out, worker_grad, job_out, job_grad = finish(home, rw, jsum, wdeg, jdeg)
    return (worker_out.T, job_out.T, worker_grad.T, job_grad.T)


def solution(mesh):
    return jax.shard_map(
        on_device,
        mesh=mesh,
        in_specs=(
            P("blk", "col"),
            P("blk", "col"),
            P("blk", "col"),
            P("blk", "col"),
            P("blk"),
            P("blk"),
            P(("blk", "col")),
            P(("blk", "col")),
            P(("blk", "col"), None, None),
            P("blk", "col"),
        ),
        out_specs=(P("blk", "col"), P("blk", "col"), P("blk", "col"), P("blk", "col")),
        check_vma=False,
    )
```
